512 devices in a mesh: dp: 64 (over y, z_lo, x), head: 8 (over z_hi, core).
Axes of the slice: x: 4, y: 4, z: 16 (z_hi: 4, z_lo: 4; z = z_hi * 4 + z_lo), core: 2. Of those that a mesh axis runs over, the one named last changes fastest.
Arguments:
- response_q: bfloat16 [16384, 5120], P(('dp', 'head')), may hold values from -90 to 90
- response_k: bfloat16 [16384, 1024], P(('dp', 'head')), may hold values from -4.5 to 4.5
- response_saved_values: bfloat16 [16384, 1024], P(('dp', 'head')), may hold values from -4.5 to 4.5
- response_o: bfloat16 [16384, 5120], P(('dp', 'head')), may hold values from -4.5 to 4.5
- response_do: bfloat16 [16384, 5120], P(('dp', 'head')), may hold values from -4.5 to 4.5
- prompt_q: bfloat16 [4096, 5120], P(('dp', 'head')), may hold values from -90 to 90
- prompt_k: bfloat16 [4096, 1024], P(('dp', 'head')), may hold values from -4.5 to 4.5
- prompt_saved_values: bfloat16 [4096, 1024], P(('dp', 'head')), may hold values from -4.5 to 4.5
- prompt_o: bfloat16 [4096, 5120], P(('dp', 'head')), may hold values from -4.5 to 4.5
- prompt_do: bfloat16 [4096, 5120], P(('dp', 'head')), may hold values from -4.5 to 4.5
- resp_len: int32 [256], replicated, may hold values from 4 to 64, as said below
- resp_prompt: int32 [256], replicated, may hold values from 0 to 15, as said below
- plan_rank: int32 [256], replicated, may hold values from 0 to 63, as said below
- plan_offset: int32 [256], replicated, may hold values from 0 to 192, as said below
Outputs:
- response_dq: bfloat16 [16384, 5120], P(('dp', 'head'))
- response_dk: bfloat16 [16384, 1024], P(('dp', 'head'))
- response_dv: bfloat16 [16384, 1024], P(('dp', 'head'))
- prompt_dq: bfloat16 [4096, 5120], P(('dp', 'head'))
- prompt_dk: bfloat16 [4096, 1024], P(('dp', 'head'))
- prompt_dv: bfloat16 [4096, 1024], P(('dp', 'head'))
The draws below stay inside these ranges and needn't reach their ends.
Inputs may be any that keep to these rules, and one draw needn't show every extreme that they name: `resp_len`: some response has exactly 64 tokens. `resp_prompt`: each prompt has 16 responses. `plan_rank`: each index of dp holds exactly four responses: two of one prompt and two of another. `plan_offset`: the responses of one index of dp fill its rows from row 0 one after another without gaps, in any order; some index of dp holds four responses of 64 tokens.
All inputs are finite; a program needn't handle non-finite values.
Results may differ from the reference program's by a relative error of at most 0.005.
Values may be sent and summed in bfloat16 or wider, within the bound.
A program may use at most 64 MiB of HBM per device.

```python
import jax
import jax.numpy as jnp
from jax import lax

QUERY_HEADS = 40
KEY_VALUE_HEADS = 8
HEAD_SIZE = 128
QUERY_PER_KV = 5
RESPONSE_ROWS = 256
PROMPT_LENGTH = 256
PROMPT_COUNT = 16
RESP_MIN = 4
RESP_MAX = 64
N_DP = 64


def packing(key):
    streams = jax.random.split(key, 6)
    firsts = jax.random.permutation(streams[0], N_DP)
    seconds = jax.random.permutation(streams[1], N_DP)
    lower = firsts // 8
    upper = PROMPT_COUNT // 2 + seconds // 8
    slot_prompt = jnp.stack([lower, lower, upper, upper], axis=1)
    orders = jax.vmap(lambda single: jax.random.permutation(single, 4))(jax.random.split(streams[2], N_DP))
    slot_prompt = jnp.take_along_axis(slot_prompt, orders, axis=1)
    lengths = jax.random.randint(streams[3], (N_DP, 4), RESP_MIN, RESP_MAX + 1)
    chosen = jax.random.randint(streams[4], (), 0, N_DP)
    lengths = jnp.where(jnp.arange(N_DP)[:, None] == chosen, RESP_MAX, lengths)
    offsets = jnp.cumsum(lengths, axis=1) - lengths
    ranks = jnp.broadcast_to(jnp.arange(N_DP)[:, None], (N_DP, 4))
    labels = jax.random.permutation(streams[5], N_DP * 4)

    def place(entries):
        return jnp.zeros((N_DP * 4,), jnp.int32).at[labels].set(entries.reshape(-1).astype(jnp.int32))
    return (place(lengths), place(slot_prompt), place(ranks), place(offsets))


def drawn_keys(key, count_of_rows, random_seed):
    base_offset = jnp.clip(jax.random.normal(jax.random.fold_in(key, random_seed), (count_of_rows, KEY_VALUE_HEADS * HEAD_SIZE), jnp.float32), -4.5, 4.5)
    return base_offset


def keys_for(key, count_of_rows, random_seed):
    base_offset = drawn_keys(key, count_of_rows, random_seed)
    return base_offset.astype(jnp.bfloat16)


def queries_for(key, count_of_rows, own):
    drawn = jnp.clip(jax.random.normal(own, (count_of_rows, QUERY_HEADS * HEAD_SIZE), jnp.float32), -4.5, 4.5)
    return drawn.astype(jnp.bfloat16)


def draw_response_k(key, part):
    result = keys_for(key, N_DP * RESPONSE_ROWS, 40)
    return result


def draw_response_q(key, part):
    own = jax.random.fold_in(key, 2)
    return queries_for(key, N_DP * RESPONSE_ROWS, own)


def draw_prompt_k(key, part):
    result = keys_for(key, PROMPT_COUNT * PROMPT_LENGTH, 60)
    return result


def draw_prompt_q(key, part):
    own = jax.random.fold_in(key, 4)
    return queries_for(key, PROMPT_COUNT * PROMPT_LENGTH, own)


def draw_resp_len(key, part):
    tables = packing(key)
    return tables[0]


def draw_resp_prompt(key, part):
    tables = packing(key)
    return tables[1]


def draw_plan_rank(key, part):
    tables = packing(key)
    return tables[2]


def draw_plan_offset(key, part):
    tables = packing(key)
    return tables[3]


def block_levels(own_key, shape, cuts, least, top_value):
    def one(position, shards_of):
        steps = jax.random.uniform(jax.random.fold_in(jax.random.fold_in(own_key, 6), position), (shards_of,), jnp.float32, least / len(cuts), top_value / len(cuts))
        return jnp.repeat(jnp.exp(steps), shape[position] // shards_of).reshape((-1,) + (1,) * (len(shape) - position - 1))

    factor_of = one(*cuts[0])
    for cut in cuts[1:]:
        factor_of = factor_of * one(*cut)
    return factor_of


def centred(stream_key, dims, width, limit, cuts=(), held_as=jnp.bfloat16):
    values = width * jax.random.normal(stream_key, dims, jnp.float32)
    if cuts:
        values = values * block_levels(stream_key, dims, cuts, -0.22, 0.18)
    return jnp.clip(values, -limit, limit).astype(held_as)


def setup_inputs(seed: int = 0) -> dict:
    key_list = jax.random.split(jax.random.key(seed), 15)
    return {
        "response_q": draw_response_q(jax.random.fold_in(key_list[14], 71), 0),
        "response_k": draw_response_k(jax.random.fold_in(key_list[14], 71), 0),
        "response_saved_values": centred(key_list[2], (N_DP * RESPONSE_ROWS, KEY_VALUE_HEADS * HEAD_SIZE), 1.0, 4.5, ((0, 512),)),
        "response_o": centred(key_list[3], (N_DP * RESPONSE_ROWS, QUERY_HEADS * HEAD_SIZE), 1.0, 4.5, ((0, 512),)),
        "response_do": centred(key_list[4], (N_DP * RESPONSE_ROWS, QUERY_HEADS * HEAD_SIZE), 1.0, 4.5, ((0, 512),)),
        "prompt_q": draw_prompt_q(jax.random.fold_in(key_list[14], 71), 0),
        "prompt_k": draw_prompt_k(jax.random.fold_in(key_list[14], 71), 0),
        "prompt_saved_values": centred(key_list[7], (PROMPT_COUNT * PROMPT_LENGTH, KEY_VALUE_HEADS * HEAD_SIZE), 1.0, 4.5, ((0, 512),)),
        "prompt_o": centred(key_list[8], (PROMPT_COUNT * PROMPT_LENGTH, QUERY_HEADS * HEAD_SIZE), 1.0, 4.5, ((0, 512),)),
        "prompt_do": centred(key_list[9], (PROMPT_COUNT * PROMPT_LENGTH, QUERY_HEADS * HEAD_SIZE), 1.0, 4.5, ((0, 512),)),
        "resp_len": draw_resp_len(jax.random.fold_in(key_list[14], 71), 0),
        "resp_prompt": draw_resp_prompt(jax.random.fold_in(key_list[14], 71), 0),
        "plan_rank": draw_plan_rank(jax.random.fold_in(key_list[14], 71), 0),
        "plan_offset": draw_plan_offset(jax.random.fold_in(key_list[14], 71), 0),
    }


MASKED_SCORE = -1.0e30


def row_tables(resp_len, resp_prompt, plan_rank, plan_offset, device, count_of_rows):
    row_ids = jnp.arange(count_of_rows, dtype=jnp.int32)
    holding = plan_rank == device
    member = holding[None, :] & (row_ids[:, None] >= plan_offset[None, :]) & (row_ids[:, None] < (plan_offset + resp_len)[None, :])
    labels = jnp.arange(1, resp_len.shape[0] + 1, dtype=jnp.int32)
    segment = jnp.sum(jnp.where(member, labels[None, :], 0), axis=1).astype(jnp.int32)
    owners = jnp.sum(jnp.where(member, resp_prompt[None, :], 0), axis=1).astype(jnp.int32)
    first_prompt = jnp.min(jnp.where(holding, resp_prompt, resp_prompt.shape[0])).astype(jnp.int32)
    last_prompt = jnp.max(jnp.where(holding, resp_prompt, 0)).astype(jnp.int32)
    return segment, owners, first_prompt, last_prompt


def response_allowed(segment, owners, first_prompt, last_prompt):
    item_count = segment.shape[0]
    row_ids = jnp.arange(item_count, dtype=jnp.int32)
    filled = segment > 0
    take_first = (owners == first_prompt) & filled
    take_last = (owners == last_prompt) & (last_prompt != first_prompt) & filled
    prefix = jnp.concatenate([jnp.broadcast_to(take_first[:, None], (item_count, PROMPT_LENGTH)), jnp.broadcast_to(take_last[:, None], (item_count, PROMPT_LENGTH))], axis=1)
    own_rows = (segment[:, None] == segment[None, :]) & filled[:, None] & (row_ids[None, :] <= row_ids[:, None])
    return jnp.concatenate([prefix, own_rows], axis=1)


def attend(query_block, key_row_block, value_row_block, attention_output, output_gradient, allowed):
    item_count = query_block.shape[0]
    count_of_keys = key_row_block.shape[0]
    scale = HEAD_SIZE ** -0.5
    query_func = query_block.astype(jnp.float32).reshape(item_count, KEY_VALUE_HEADS, QUERY_PER_KV, HEAD_SIZE)
    key_func = key_row_block.astype(jnp.float32).reshape(count_of_keys, KEY_VALUE_HEADS, HEAD_SIZE)
    value_func = value_row_block.astype(jnp.float32).reshape(count_of_keys, KEY_VALUE_HEADS, HEAD_SIZE)
    output_func = attention_output.astype(jnp.float32).reshape(item_count, KEY_VALUE_HEADS, QUERY_PER_KV, HEAD_SIZE)
    gradient_func = output_gradient.astype(jnp.float32).reshape(item_count, KEY_VALUE_HEADS, QUERY_PER_KV, HEAD_SIZE)
    scores = jnp.einsum('qgjd,kgd->gjqk', query_func, key_func) * scale
    seen = allowed[None, None]
    masked = jnp.where(seen, scores, MASKED_SCORE)
    highest = jnp.max(masked, axis=-1, keepdims=True)
    totals = jnp.sum(jnp.where(seen, jnp.exp(masked - highest), 0.0), axis=-1, keepdims=True)
    empty_row = jnp.where(jnp.any(allowed, axis=-1)[None, None, :, None], 0.0, 1.0)
    log_total = highest + jnp.log(totals + empty_row)
    likely = jnp.where(seen, jnp.exp(scores - log_total), 0.0)
    weights = lax.optimization_barrier(likely.astype(jnp.bfloat16)).astype(jnp.float32)
    deltas = jnp.sum(output_func * gradient_func, axis=-1).transpose(1, 2, 0)
    prob_grad = jnp.einsum('qgjd,kgd->gjqk', gradient_func, value_func)
    score_grad = lax.optimization_barrier((likely * (prob_grad - deltas[..., None])).astype(jnp.bfloat16)).astype(jnp.float32)
    query_gradient = jnp.einsum('gjqk,kgd->qgjd', score_grad, key_func) * scale
    key_gradient = jnp.einsum('gjqk,qgjd->kgd', score_grad, query_func) * scale
    value_gradient = jnp.einsum('gjqk,qgjd->kgd', weights, gradient_func)
    return query_gradient.reshape(item_count, QUERY_HEADS * HEAD_SIZE), key_gradient.reshape(count_of_keys, KEY_VALUE_HEADS * HEAD_SIZE), value_gradient.reshape(count_of_keys, KEY_VALUE_HEADS * HEAD_SIZE)


def reference(response_q, response_k, response_saved_values, response_o, response_do, prompt_q, prompt_k, prompt_saved_values, prompt_o, prompt_do, resp_len, resp_prompt, plan_rank, plan_offset):
    key_value_width = KEY_VALUE_HEADS * HEAD_SIZE

    def per_rank(carried, device):
        total_key, total_value = carried
        segment, owners, first_prompt, last_prompt = row_tables(resp_len, resp_prompt, plan_rank, plan_offset, device, RESPONSE_ROWS)
        start = (device * RESPONSE_ROWS).astype(jnp.int32)

        def take(source):
            return lax.dynamic_slice_in_dim(source, start, RESPONSE_ROWS, 0)

        first_start = (first_prompt * PROMPT_LENGTH).astype(jnp.int32)
        last_start = (last_prompt * PROMPT_LENGTH).astype(jnp.int32)
        key_row_block = jnp.concatenate([lax.dynamic_slice_in_dim(prompt_k, first_start, PROMPT_LENGTH, 0), lax.dynamic_slice_in_dim(prompt_k, last_start, PROMPT_LENGTH, 0), take(response_k)], axis=0)
        value_row_block = jnp.concatenate([lax.dynamic_slice_in_dim(prompt_saved_values, first_start, PROMPT_LENGTH, 0), lax.dynamic_slice_in_dim(prompt_saved_values, last_start, PROMPT_LENGTH, 0), take(response_saved_values)], axis=0)
        allowed = response_allowed(segment, owners, first_prompt, last_prompt)
        query_gradient, key_gradient, value_gradient = attend(take(response_q), key_row_block, value_row_block, take(response_o), take(response_do), allowed)
        total_key = lax.dynamic_update_slice_in_dim(total_key, lax.dynamic_slice_in_dim(total_key, first_start, PROMPT_LENGTH, 0) + key_gradient[:PROMPT_LENGTH], first_start, 0)
        total_key = lax.dynamic_update_slice_in_dim(total_key, lax.dynamic_slice_in_dim(total_key, last_start, PROMPT_LENGTH, 0) + key_gradient[PROMPT_LENGTH:2 * PROMPT_LENGTH], last_start, 0)
        total_value = lax.dynamic_update_slice_in_dim(total_value, lax.dynamic_slice_in_dim(total_value, first_start, PROMPT_LENGTH, 0) + value_gradient[:PROMPT_LENGTH], first_start, 0)
        total_value = lax.dynamic_update_slice_in_dim(total_value, lax.dynamic_slice_in_dim(total_value, last_start, PROMPT_LENGTH, 0) + value_gradient[PROMPT_LENGTH:2 * PROMPT_LENGTH], last_start, 0)
        return (total_key, total_value), (query_gradient.astype(jnp.bfloat16), key_gradient[2 * PROMPT_LENGTH:].astype(jnp.bfloat16), value_gradient[2 * PROMPT_LENGTH:].astype(jnp.bfloat16))

    zero_rows = jnp.zeros((PROMPT_COUNT * PROMPT_LENGTH, key_value_width), jnp.float32)
    (total_key, total_value), (rows_dq, rows_dk, rows_dv) = lax.scan(per_rank, (zero_rows, zero_rows), jnp.arange(N_DP, dtype=jnp.int32))
    col_ids = jnp.arange(PROMPT_LENGTH, dtype=jnp.int32)
    causal = col_ids[None, :] <= col_ids[:, None]

    def per_prompt(prompt_id):
        start = (prompt_id * PROMPT_LENGTH).astype(jnp.int32)

        def take(source):
            return lax.dynamic_slice_in_dim(source, start, PROMPT_LENGTH, 0)

        return attend(take(prompt_q), take(prompt_k), take(prompt_saved_values), take(prompt_o), take(prompt_do), causal)

    lead_dq, lead_dk, lead_dv = lax.map(per_prompt, jnp.arange(PROMPT_COUNT, dtype=jnp.int32))
    prompt_dk = (total_key + lead_dk.reshape(PROMPT_COUNT * PROMPT_LENGTH, key_value_width)).astype(jnp.bfloat16)
    prompt_dv = (total_value + lead_dv.reshape(PROMPT_COUNT * PROMPT_LENGTH, key_value_width)).astype(jnp.bfloat16)
    return (rows_dq.reshape(N_DP * RESPONSE_ROWS, QUERY_HEADS * HEAD_SIZE), rows_dk.reshape(N_DP * RESPONSE_ROWS, key_value_width), rows_dv.reshape(N_DP * RESPONSE_ROWS, key_value_width), lead_dq.reshape(PROMPT_COUNT * PROMPT_LENGTH, QUERY_HEADS * HEAD_SIZE).astype(jnp.bfloat16), prompt_dk, prompt_dv)
```

```python
import jax
import jax.numpy as jnp
from jax import lax
from jax.experimental import pallas as pl
from jax.experimental.pallas import tpu as pltpu
from jax.sharding import PartitionSpec as P

D = 128
QPK = 5
W = QPK * D
PROMPT = 256
MASKED = -1e30
SCALE = D**-0.5
MESH = pl.DeviceIdType.MESH
BF = jnp.bfloat16
F32 = jnp.float32


def coords():
    dp = lax.axis_index("dp")
    hd = lax.axis_index("head")
    x, zl, y = lax.rem(dp, 4), lax.rem(dp // 4, 4), dp // 16
    zh, c = hd // 2, lax.rem(hd, 2)
    return x, y, zh * 4 + zl, c


def place(x, y, z, c):
    return ((y * 4 + lax.rem(z, 4)) * 4 + x, (z // 4) * 2 + c)


def wrap(a, n):
    return lax.rem(a + 4 * n, n)


def remote(src, dst, send_sem, recv_sem, device):
    return pltpu.make_async_remote_copy(
        src_ref=src,
        dst_ref=dst,
        send_sem=send_sem,
        recv_sem=recv_sem,
        device_id=device,
        device_id_type=MESH,
    )


class Peers:
    def __init__(self):
        self.x, self.y, self.z, self.c = coords()
        self.s = 2 * self.x + self.c
        x, y, z, c, s = self.x, self.y, self.z, self.c, self.s
        self.group = [wrap(s + d, 8) for d in range(1, 8)]
        self.group_dev = [place(g // 2, y, z, lax.rem(g, 2)) for g in self.group]
        self.sender = [wrap(s - d, 8) for d in range(1, 8)]
        self.y_dev = [place(x, wrap(y + d, 4), z, c) for d in range(1, 4)]
        self.up = place(x, y, wrap(z + 1, 16), c)
        self.down = place(x, y, wrap(z - 1, 16), c)
        self.up4 = place(x, y, wrap(z + 4, 16), c)
        self.down4 = place(x, y, wrap(z - 4, 16), c)

    def signal_all(self):
        barrier = pltpu.get_barrier_semaphore()
        peers = [*self.group_dev, *self.y_dev, self.up, self.down, self.up4, self.down4]
        for peer in peers:
            pl.semaphore_signal(barrier, inc=1, device_id=peer, device_id_type=MESH)
        return barrier, len(peers)


def head_sums(o_ref, do_ref, rows):
    lane = lax.broadcasted_iota(jnp.int32, (rows, D), 1)
    total = jnp.zeros((rows, D), F32)
    for g in range(8 * QPK):
        cols = slice(g * D, (g + 1) * D)
        one = jnp.sum(o_ref[:, cols].astype(F32) * do_ref[:, cols].astype(F32), axis=1, keepdims=True)
        total = jnp.where(lane == g, one, total)
    return total


def gather_kernel(
    rq, rk, rv, ro, rdo, pq, pk, pv, po, pdo,
    rq_o, rdo_o, rkv_o, prev_o, g_o, pqd_o, dl_o,
    pkv_s, pqd_s, dl_s,
    a_send, a_recv, own_sem, sh_send, sh_recv, r_send, r_recv, l_send, l_recv, y_send, y_recv,
):
    me = Peers()
    s, y, z = me.s, me.y, me.z
    barrier, count = me.signal_all()
    for g in range(8):
        k8 = pk[:, g * D : (g + 1) * D].astype(F32)
        v8 = pv[:, g * D : (g + 1) * D].astype(F32)
        pkv_s[g] = jnp.concatenate([k8, v8], axis=0).astype(BF)
    for g in range(8):
        parts = [pq[:, (g * QPK + i) * D : (g * QPK + i + 1) * D].astype(F32) for i in range(QPK)]
        parts += [pdo[:, (g * QPK + i) * D : (g * QPK + i + 1) * D].astype(F32) for i in range(QPK)]
        pqd_s[g] = jnp.concatenate(parts, axis=0).astype(BF)
    sums = jnp.concatenate(
        [head_sums(ro, rdo, 32), head_sums(po, pdo, 8), jnp.zeros((D - 40, D), F32)], axis=0
    ).T
    for g in range(8):
        dl_s[g, 0:QPK, :] = sums[g * QPK : (g + 1) * QPK, :]
        dl_s[g, QPK:8, :] = jnp.zeros((8 - QPK, D), F32)
    pl.semaphore_wait(barrier, count)

    def cols(ref, h, width):
        return ref.at[:, pl.ds(pl.multiple_of(h * width, D), width)]

    mine = (y * 4 + lax.rem(z, 4), z // 4)
    sources = [
        lambda h: pkv_s.at[h],
        lambda h: cols(rk, h, D),
        lambda h: cols(rv, h, D),
        lambda h: cols(rq, h, W),
        lambda h: cols(rdo, h, W),
        lambda h: pqd_s.at[h],
        lambda h: dl_s.at[h],
    ]
    landing = [
        lambda j: g_o.at[mine[0], mine[1], j],
        lambda j: rkv_o.at[0, j],
        lambda j: rkv_o.at[1, j],
        lambda j: rq_o.at[j],
        lambda j: rdo_o.at[j],
        lambda j: pqd_o.at[j],
        lambda j: dl_o.at[j],
    ]
    kinds = range(len(sources))
    own = [pltpu.make_async_copy(sources[n](s), landing[n](s), own_sem.at[n]) for n in kinds]
    sent = []
    for n in kinds:
        own[n].start()
        for d in range(7):
            h = me.group[d]
            copy = remote(sources[n](h), landing[n](s), a_send.at[n, d], a_recv.at[n, s], me.group_dev[d])
            copy.start()
            sent.append(copy)

    def arrived(n):
        own[n].wait()
        for d in range(7):
            j = me.sender[d]
            remote(landing[n](j), landing[n](j), a_send.at[n, d], a_recv.at[n, j], me.group_dev[d]).wait_recv()

    def block(yy, zz):
        return g_o.at[yy * 4 + lax.rem(zz, 4), zz // 4]

    def spread(zz):
        for d in range(3):
            copy = remote(block(y, zz), block(y, zz), y_send.at[zz, d], y_recv.at[zz, d], me.y_dev[d])
            copy.start()
            sent.append(copy)

    arrived(0)
    for t in range(9):
        zr, zl = wrap(z - t, 16), wrap(z + t, 16)
        if t > 0:
            remote(block(y, zr), block(y, zr), r_send.at[t - 1], r_recv.at[t - 1], me.up).wait_recv()
        if t < 8:
            copy = remote(block(y, zr), block(y, zr), r_send.at[t], r_recv.at[t], me.up)
            copy.start()
            sent.append(copy)
        if 0 < t < 8:
            remote(block(y, zl), block(y, zl), l_send.at[t - 1], l_recv.at[t - 1], me.down).wait_recv()
        if t < 7:
            copy = remote(block(y, zl), block(y, zl), l_send.at[t], l_recv.at[t], me.down)
            copy.start()
            sent.append(copy)
        spread(zr)
        if 0 < t < 8:
            spread(zl)
        if t == 1:
            arrived(1)
            arrived(2)
            shift = remote(rkv_o, prev_o, sh_send, sh_recv, me.up4)
            shift.start()
    for n in range(3, len(sources)):
        arrived(n)
    shift.wait()
    for zz in range(16):
        for d in range(3):
            there = block(wrap(y - d - 1, 4), zz)
            remote(there, there, y_send.at[zz, d], y_recv.at[zz, d], me.y_dev[d]).wait_recv()
    for copy in sent:
        copy.wait_send()


def dot_t(a, b):
    return lax.dot_general(a, b, (((1,), (1,)), ((), ())), preferred_element_type=F32)


def dot(a, b):
    return lax.dot_general(a, b, (((1,), (0,)), ((), ())), preferred_element_type=F32)


def t_dot(a, b):
    return lax.dot_general(a, b, (((0,), (0,)), ((), ())), preferred_element_type=F32)


def grads(q, do, delta, k, v, bias, filled):
    scores = dot_t(q, k) * SCALE + bias
    highest = jnp.max(scores, axis=1, keepdims=True)
    e = jnp.exp(scores - highest)
    total = jnp.sum(e, axis=1, keepdims=True)
    likely = e * jnp.where(filled, 1.0 / total, 0.0)
    prob_grad = dot_t(do, v)
    score_grad = (likely * (prob_grad - delta)).astype(BF)
    dq = dot(score_grad, k) * SCALE
    dk = t_dot(score_grad, q) * SCALE
    dv = t_dot(likely.astype(BF), do)
    return dq, dk, dv


def compute_kernel(
    tab, rq, rdo, rkv, prev, g, pqd, dl,
    dq_o, cur_o, prev_d, dense_o, pdq_o,
    acc,
):
    x, y, z, c = coords()
    zl, zh = lax.rem(z, 4), z // 4
    acc[...] = jnp.zeros_like(acc)
    tab_row = tab[...].astype(F32)
    tab_col = tab_row.T

    def stack(parts):
        return jnp.concatenate(parts, axis=0)

    def prompt_rows(p):
        kv = g[p].astype(F32)
        return kv[:, 0:8, :].reshape(PROMPT, D).astype(BF), kv[:, 8:16, :].reshape(PROMPT, D).astype(BF)

    def add(p, dk, dv):
        acc[p, :, 0:8, :] += dk.reshape(32, 8, D)
        acc[p, :, 8:16, :] += dv.reshape(32, 8, D)

    def one_rank(r, _):
        rank = ((y * 4 + zl) * 4 + r).astype(F32)
        base = zh * 64
        holding = tab_row[2:3, :] == rank
        owner = tab_row[1:2, :]
        first_f = jnp.min(jnp.where(holding, owner, 16.0))
        last_f = jnp.max(jnp.where(holding, owner, 0.0))
        first, last = first_f.astype(jnp.int32), last_f.astype(jnp.int32)
        row = (lax.broadcasted_iota(jnp.int32, (64, PROMPT), 0) + base).astype(F32)
        label = (lax.broadcasted_iota(jnp.int32, (64, PROMPT), 1) + 1).astype(F32)
        start, stop = tab_row[3:4, :], tab_row[3:4, :] + tab_row[0:1, :]
        member = holding & (row >= start) & (row < stop)
        seg_q = jnp.sum(jnp.where(member, label, 0.0), axis=1, keepdims=True)
        owner_q = jnp.sum(jnp.where(member, jnp.broadcast_to(owner, member.shape), 0.0), axis=1, keepdims=True)
        key_row = (lax.broadcasted_iota(jnp.int32, (PROMPT, D), 1) + base - 64).astype(F32)
        key_label = (lax.broadcasted_iota(jnp.int32, (PROMPT, D), 0) + 1).astype(F32)
        start_c, stop_c = tab_col[:, 3:4], tab_col[:, 3:4] + tab_col[:, 0:1]
        key_member = (tab_col[:, 2:3] == rank) & (key_row >= start_c) & (key_row < stop_c)
        seg_k = jnp.sum(jnp.where(key_member, key_label, 0.0), axis=0, keepdims=True)
        filled = seg_q > 0.0
        q_pos = lax.broadcasted_iota(jnp.int32, (64, D), 0) + 64
        k_pos = lax.broadcasted_iota(jnp.int32, (64, D), 1)
        own = (seg_q == seg_k) & filled & (k_pos <= q_pos)
        take_first = filled & (owner_q == first_f)
        take_last = filled & (owner_q == last_f) & (first_f != last_f)
        bias = jnp.concatenate(
            [
                jnp.broadcast_to(jnp.where(take_first, 0.0, MASKED), (64, PROMPT)),
                jnp.broadcast_to(jnp.where(take_last, 0.0, MASKED), (64, PROMPT)),
                jnp.where(own, 0.0, MASKED),
            ],
            axis=1,
        )
        bias = stack([bias] * QPK)
        filled5 = stack([jnp.where(filled, 1.0, 0.0)] * QPK) > 0.0
        two = pl.ds(2 * r, 2)
        q2 = rq[two].reshape(64, W)
        do2 = rdo[two].reshape(64, W)
        q = stack([q2[:, i * D : (i + 1) * D] for i in range(QPK)])
        do = stack([do2[:, i * D : (i + 1) * D] for i in range(QPK)])
        dl2 = dl[two]
        dl0, dl1 = dl2[0].T, dl2[1].T
        delta = stack([part[0:32, i : i + 1] for i in range(QPK) for part in (dl0, dl1)])
        k1, v1 = prompt_rows(first)
        k2, v2 = prompt_rows(last)
        k = stack([k1, k2, prev[0, two].reshape(64, D), rkv[0, two].reshape(64, D)])
        v = stack([v1, v2, prev[1, two].reshape(64, D), rkv[1, two].reshape(64, D)])
        dq, dk, dv = grads(q, do, delta, k, v, bias, filled5)
        dq = dq.astype(BF)
        dq_o[two] = jnp.concatenate([dq[i * 64 : (i + 1) * 64] for i in range(QPK)], axis=1).reshape(2, 32, W)
        add(first, dk[0:256], dv[0:256])
        add(last, dk[256:512], dv[256:512])
        prev_d[0, two] = dk[512:576].astype(BF).reshape(2, 32, D)
        prev_d[1, two] = dv[512:576].astype(BF).reshape(2, 32, D)
        cur_o[0, two] = dk[576:640].reshape(2, 32, D)
        cur_o[1, two] = dv[576:640].reshape(2, 32, D)
        return 0

    lax.fori_loop(0, 4, one_rank, 0)

    p = y * 4 + zl
    lead = pqd[...].astype(F32)
    q = stack([lead[:, i * 8 : i * 8 + 8, :].reshape(64, D) for i in range(QPK)]).astype(BF)
    do = stack([lead[:, (i + 5) * 8 : (i + 5) * 8 + 8, :].reshape(64, D) for i in range(QPK)]).astype(BF)
    dls = [dl[j].T for j in range(8)]
    delta = stack([dls[j][32:40, i : i + 1] for i in range(QPK) for j in range(8)])

    def place_of(n, hi):
        j, i = (n // 8) % 8, n % 8
        return (j // 2) * 64 + (hi * 2 + j % 2) * 8 + i

    n_q = lax.broadcasted_iota(jnp.int32, (64, PROMPT), 0)
    n_k = lax.broadcasted_iota(jnp.int32, (64, PROMPT), 1)
    bias = jnp.where(place_of(n_k, n_k // 64) <= place_of(n_q, zh), 0.0, MASKED)
    k, v = prompt_rows(p)
    dq, dk, dv = grads(q, do, delta, k, v, stack([bias] * QPK), True)
    add(p, dk, dv)
    for j in range(8):
        tiles = [dq[i * 64 + j * 8 : i * 64 + j * 8 + 8] for i in range(QPK)]
        pdq_o[j] = stack([*tiles, jnp.zeros((8, D), F32)]).astype(BF)
    dense_o[...] = acc[...].astype(BF)


def scatter_kernel(
    dq, cur, prev_d, dense, pdq,
    dq_o, dk_o, dv_o, pdq_o, pdk_o, pdv_o,
    back, y_in, r_out, r_in, l_out, l_in, kv_s, pkv_s, pdq_in, pkv_in,
    a_send, a_recv, own_sem, sh_send, sh_recv, r_send, r_recv, l_send, l_recv, y_send, y_recv,
):
    me = Peers()
    s, y, z = me.s, me.y, me.z
    barrier, count = me.signal_all()
    pl.semaphore_wait(barrier, count)
    sent = []

    def cols(ref, h, width):
        return ref.at[:, pl.ds(pl.multiple_of(h * width, D), width)]

    def block(yy, zz):
        return (yy * 4 + lax.rem(zz, 4), zz // 4)

    order = []
    for t in range(8):
        order.append(8 - t)
        if t < 7:
            order.append(-7 + t)
    order.append(0)
    targets = {k: wrap(z + k, 16) for k in order}

    def exchange(k):
        zz = targets[k]
        for d in range(3):
            there = block(wrap(y + d + 1, 4), zz)
            copy = remote(dense.at[there[0], there[1]], y_in.at[d, zz], y_send.at[zz, d], y_recv.at[zz, d], me.y_dev[d])
            copy.start()
            sent.append(copy)

    for k in order[:4]:
        exchange(k)
    shift = remote(prev_d, back, sh_send, sh_recv, me.down4)
    shift.start()
    for k in order[4:]:
        exchange(k)

    sources = [
        lambda h: dq.at[h],
        lambda h: pdq.at[h],
        lambda h: kv_s.at[0, h],
        lambda h: kv_s.at[1, h],
        lambda h: pkv_s.at[h],
    ]
    landing = [
        lambda j: cols(dq_o, j, W),
        lambda j: pdq_in.at[j],
        lambda j: cols(dk_o, j, D),
        lambda j: cols(dv_o, j, D),
        lambda j: pkv_in.at[j],
    ]
    own = {}

    def send(n):
        own[n] = pltpu.make_async_copy(sources[n](s), landing[n](s), own_sem.at[n])
        own[n].start()
        for d in range(7):
            h = me.group[d]
            copy = remote(sources[n](h), landing[n](s), a_send.at[n, d], a_recv.at[n, s], me.group_dev[d])
            copy.start()
            sent.append(copy)

    def arrived(n):
        own[n].wait()
        for d in range(7):
            j = me.sender[d]
            remote(landing[n](j), landing[n](j), a_send.at[n, d], a_recv.at[n, j], me.group_dev[d]).wait_recv()

    send(0)
    send(1)

    def partial(k):
        zz = targets[k]
        here = block(y, zz)
        total = dense[here[0], here[1]].astype(F32)
        for d in range(3):
            remote(y_in.at[d, zz], y_in.at[d, zz], y_send.at[zz, d], y_recv.at[zz, d], me.y_dev[d]).wait_recv()
            total += y_in[d, zz].astype(F32)
        return total

    def r_arrival(t):
        remote(r_in.at[t], r_in.at[t], r_send.at[t], r_recv.at[t], me.up).wait_recv()
        return r_in[t].astype(F32)

    def l_arrival(t):
        remote(l_in.at[t], l_in.at[t], l_send.at[t], l_recv.at[t], me.down).wait_recv()
        return l_in[t].astype(F32)

    for t in range(8):
        total = partial(8 - t)
        if t > 0:
            total += r_arrival(t - 1)
        r_out[t] = total.astype(BF)
        copy = remote(r_out.at[t], r_in.at[t], r_send.at[t], r_recv.at[t], me.up)
        copy.start()
        sent.append(copy)
        if t < 7:
            total = partial(-7 + t)
            if t > 0:
                total += l_arrival(t - 1)
            l_out[t] = total.astype(BF)
            copy = remote(l_out.at[t], l_in.at[t], l_send.at[t], l_recv.at[t], me.down)
            copy.start()
            sent.append(copy)
        if t == 4:
            shift.wait_recv()
            kv_s[...] = (cur[...] + back[...].astype(F32)).astype(BF)
            send(2)
            send(3)
    total = partial(0) + r_arrival(7) + l_arrival(6)
    pkv_s[...] = total.astype(BF)
    send(4)
    arrived(1)
    for h in range(8):
        tiles = pdq_in[h].astype(F32)
        for i in range(QPK):
            pdq_o[:, (h * QPK + i) * D : (h * QPK + i + 1) * D] = tiles[i * 8 : i * 8 + 8].astype(BF)
    arrived(0)
    arrived(2)
    arrived(3)
    arrived(4)
    for h in range(8):
        tile = pkv_in[h].astype(F32)
        pdk_o[:, h * D : (h + 1) * D] = tile[0:8].astype(BF)
        pdv_o[:, h * D : (h + 1) * D] = tile[8:16].astype(BF)
    shift.wait_send()
    for copy in sent:
        copy.wait_send()


def vmem(n):
    return [pl.BlockSpec(memory_space=pltpu.VMEM)] * n


def shapes(*items):
    return [jax.ShapeDtypeStruct(shape, dtype) for shape, dtype in items]


def local(
    response_q, response_k, response_v, response_o, response_do,
    prompt_q, prompt_k, prompt_v, prompt_o, prompt_do,
    resp_len, resp_prompt, plan_rank, plan_offset,
):
    dma = pltpu.SemaphoreType.DMA
    limit = 40 * 2**20
    rq, rdo, rkv, prev, g, pqd, dl = pl.pallas_call(
        gather_kernel,
        out_shape=shapes(
            ((8, 32, W), BF),
            ((8, 32, W), BF),
            ((2, 8, 32, D), BF),
            ((2, 8, 32, D), BF),
            ((16, 4, 8, 16, D), BF),
            ((8, 80, D), BF),
            ((8, 8, D), F32),
        ),
        in_specs=vmem(10),
        out_specs=vmem(7),
        scratch_shapes=[
            pltpu.VMEM((8, 16, D), BF),
            pltpu.VMEM((8, 80, D), BF),
            pltpu.VMEM((8, 8, D), F32),
            dma((7, 7)),
            dma((7, 8)),
            dma((7,)),
            dma,
            dma,
            dma((8,)),
            dma((8,)),
            dma((7,)),
            dma((7,)),
            dma((16, 3)),
            dma((16, 3)),
        ],
        compiler_params=pltpu.CompilerParams(collective_id=0, has_side_effects=True, vmem_limit_bytes=limit),
        name="exchange_in",
    )(
        response_q, response_k, response_v, response_o, response_do,
        prompt_q, prompt_k, prompt_v, prompt_o, prompt_do,
    )
    zero = jnp.zeros_like(resp_len)
    tab = jnp.stack([resp_len, resp_prompt, plan_rank, plan_offset, zero, zero, zero, zero])
    dq, cur, prev_d, dense, pdq = pl.pallas_call(
        compute_kernel,
        out_shape=shapes(
            ((8, 32, W), BF),
            ((2, 8, 32, D), F32),
            ((2, 8, 32, D), BF),
            ((16, 32, 16, D), BF),
            ((8, 48, D), BF),
        ),
        in_specs=vmem(8),
        out_specs=vmem(5),
        scratch_shapes=[pltpu.VMEM((16, 32, 16, D), F32)],
        compiler_params=pltpu.CompilerParams(vmem_limit_bytes=limit),
        name="attention_grads",
    )(tab, rq, rdo, rkv, prev, g.reshape(16, 32, 16, D), pqd, dl)
    return tuple(
        pl.pallas_call(
            scatter_kernel,
            out_shape=shapes(
                ((32, 40 * D), BF),
                ((32, 8 * D), BF),
                ((32, 8 * D), BF),
                ((8, 40 * D), BF),
                ((8, 8 * D), BF),
                ((8, 8 * D), BF),
            ),
            in_specs=vmem(5),
            out_specs=vmem(6),
            scratch_shapes=[
                pltpu.VMEM((2, 8, 32, D), BF),
                pltpu.VMEM((3, 16, 8, 16, D), BF),
                pltpu.VMEM((8, 8, 16, D), BF),
                pltpu.VMEM((8, 8, 16, D), BF),
                pltpu.VMEM((7, 8, 16, D), BF),
                pltpu.VMEM((7, 8, 16, D), BF),
                pltpu.VMEM((2, 8, 32, D), BF),
                pltpu.VMEM((8, 16, D), BF),
                pltpu.VMEM((8, 48, D), BF),
                pltpu.VMEM((8, 16, D), BF),
                dma((5, 7)),
                dma((5, 8)),
                dma((5,)),
                dma,
                dma,
                dma((8,)),
                dma((8,)),
                dma((7,)),
                dma((7,)),
                dma((16, 3)),
                dma((16, 3)),
            ],
            compiler_params=pltpu.CompilerParams(collective_id=1, has_side_effects=True, vmem_limit_bytes=limit),
            name="exchange_out",
        )(dq, cur, prev_d, dense.reshape(16, 4, 8, 16, D), pdq)
    )


def solution(mesh):
    rows = P(("dp", "head"), None)
    return jax.shard_map(
        local,
        mesh=mesh,
        in_specs=(rows,) * 10 + (P(),) * 4,
        out_specs=(rows,) * 6,
        check_vma=False,
    )
```

```python
import jax
import jax.numpy as jnp
from jax import lax
from jax.experimental import pallas as pl
from jax.experimental.pallas import tpu as pltpu
from jax.sharding import PartitionSpec as P

D = 128
QPK = 5
W = QPK * D
PROMPT = 256
MASKED = -1e30
SCALE = D**-0.5
STEP = (0, 4, -4, 8)
NEAR = (0, 1, 2, -1)
MESH = pl.DeviceIdType.MESH
BF = jnp.bfloat16
F32 = jnp.float32


def coords():
    dp = lax.axis_index("dp")
    hd = lax.axis_index("head")
    x, zl, y = lax.rem(dp, 4), lax.rem(dp // 4, 4), dp // 16
    zh, c = hd // 2, lax.rem(hd, 2)
    return x, y, zh * 4 + zl, c


def place(x, y, z, c):
    return ((y * 4 + lax.rem(z, 4)) * 4 + x, (z // 4) * 2 + c)


def wrap(a, n):
    return lax.rem(a + 4 * n, n)


def remote(src, dst, send_sem, recv_sem, device):
    return pltpu.make_async_remote_copy(
        src_ref=src,
        dst_ref=dst,
        send_sem=send_sem,
        recv_sem=recv_sem,
        device_id=device,
        device_id_type=MESH,
    )


class Peers:
    def __init__(self):
        self.x, self.y, self.z, self.c = coords()
        self.s = 2 * self.x + self.c
        x, y, z, c, s = self.x, self.y, self.z, self.c, self.s
        self.group = [wrap(s + d, 8) for d in range(1, 8)]
        self.group_dev = [place(g // 2, y, z, lax.rem(g, 2)) for g in self.group]
        self.sender = [wrap(s - d, 8) for d in range(1, 8)]
        self.y_dev = [place(x, wrap(y + d, 4), z, c) for d in range(1, 4)]
        self.up = place(x, y, wrap(z + 1, 16), c)
        self.down = place(x, y, wrap(z - 1, 16), c)
        self.up4 = place(x, y, wrap(z + 4, 16), c)
        self.down4 = place(x, y, wrap(z - 4, 16), c)
        self.z_near = [self.z_dev(k) for k in (1, -1, 2, -2, 4, -4, 8)]

    def z_dev(self, k):
        return place(self.x, self.y, wrap(self.z + k, 16), self.c)

    def signal_all(self):
        barrier = pltpu.get_barrier_semaphore()
        peers = [*self.group_dev, *self.y_dev, *self.z_near]
        for peer in peers:
            pl.semaphore_signal(barrier, inc=1, device_id=peer, device_id_type=MESH)
        return barrier, len(peers)


def head_sums(o_ref, do_ref, rows):
    lane = lax.broadcasted_iota(jnp.int32, (rows, D), 1)
    total = jnp.zeros((rows, D), F32)
    for g in range(8 * QPK):
        cols = slice(g * D, (g + 1) * D)
        one = jnp.sum(o_ref[:, cols].astype(F32) * do_ref[:, cols].astype(F32), axis=1, keepdims=True)
        total = jnp.where(lane == g, one, total)
    return total


def dot_t(a, b):
    return lax.dot_general(a, b, (((1,), (1,)), ((), ())), preferred_element_type=F32)


def dot(a, b):
    return lax.dot_general(a, b, (((1,), (0,)), ((), ())), preferred_element_type=F32)


def t_dot(a, b):
    return lax.dot_general(a, b, (((0,), (0,)), ((), ())), preferred_element_type=F32)


def grads(q, do, delta, k, v, bias, filled):
    scores = dot_t(q, k) * SCALE + bias
    highest = jnp.max(scores, axis=1, keepdims=True)
    e = jnp.exp(scores - highest)
    total = jnp.sum(e, axis=1, keepdims=True)
    likely = e * jnp.where(filled, 1.0 / total, 0.0)
    prob_grad = dot_t(do, v)
    score_grad = (likely * (prob_grad - delta)).astype(BF)
    dq = dot(score_grad, k) * SCALE
    dk = t_dot(score_grad, q) * SCALE
    dv = t_dot(likely.astype(BF), do)
    return dq, dk, dv


def main_kernel(
    rq, rk, rv, ro, rdo, pq, pk, pv, po, pdo, resp_len, resp_prompt, plan_rank, plan_offset,
    dq_o, dk_o, dv_o, pdq_in, pkv_in,
    ro_s, rdo_s, pq_s, pk_s, pv_s, po_s, pdo_s, tab_s, pkv_s, pqd_s, dl_s,
    rq_in, rdo_in, rkv, prev, g_in, pqd, dl,
    bias_s, filled_s, part, dq_s, cur, prev_d, pdq,
    back, y_out, y_in, own_sum, n_out, n_in, f_out, f_in, kv_s, pkvo_s,
    load_sem, a_send, a_recv, own_sem, sh_send, sh_recv,
    f_send, f_recv, n_send, n_recv, y_send, y_recv,
    ao_send, ao_recv, owno_sem, sho_send, sho_recv,
    fo_send, fo_recv, no_send, no_recv, yo_send, yo_recv,
):
    me = Peers()
    s, y, z = me.s, me.y, me.z
    barrier, count = me.signal_all()
    pairs = [(pk, pk_s), (pv, pv_s), (pq, pq_s), (pdo, pdo_s), (po, po_s), (ro, ro_s), (rdo, rdo_s)]
    loads = [pltpu.make_async_copy(src, dst, load_sem.at[n]) for n, (src, dst) in enumerate(pairs)]
    for load in loads:
        load.start()
    for n, table in enumerate((resp_len, resp_prompt, plan_rank, plan_offset)):
        loads.append(pltpu.make_async_copy(table, tab_s.at[n : n + 1], load_sem.at[7 + n]))
        loads[-1].start()
    loads[0].wait()
    loads[1].wait()
    for g in range(8):
        k8 = pk_s[:, g * D : (g + 1) * D].astype(F32)
        v8 = pv_s[:, g * D : (g + 1) * D].astype(F32)
        pkv_s[g] = jnp.concatenate([k8, v8], axis=0).astype(BF)
    pl.semaphore_wait(barrier, count)

    def masks():
        zh = z // 4
        tab_s[4:8, :] = jnp.zeros((4, 256), jnp.int32)
        tab_row = tab_s[...].astype(F32)
        tab_col = tab_row.T

        def one(r, _):
            rank = ((y * 4 + lax.rem(z, 4)) * 4 + r).astype(F32)
            base = zh * 64
            holding = tab_row[2:3, :] == rank
            owner = tab_row[1:2, :]
            first = jnp.min(jnp.where(holding, owner, 16.0), axis=1, keepdims=True)
            last = jnp.max(jnp.where(holding, owner, 0.0), axis=1, keepdims=True)
            row = (lax.broadcasted_iota(jnp.int32, (64, PROMPT), 0) + base).astype(F32)
            label = (lax.broadcasted_iota(jnp.int32, (64, PROMPT), 1) + 1).astype(F32)
            start, stop = tab_row[3:4, :], tab_row[3:4, :] + tab_row[0:1, :]
            member = holding & (row >= start) & (row < stop)
            seg_q = jnp.sum(jnp.where(member, label, 0.0), axis=1, keepdims=True)
            owner_q = jnp.sum(jnp.where(member, jnp.broadcast_to(owner, member.shape), 0.0), axis=1, keepdims=True)
            key_row = (lax.broadcasted_iota(jnp.int32, (PROMPT, D), 1) + base - 64).astype(F32)
            key_label = (lax.broadcasted_iota(jnp.int32, (PROMPT, D), 0) + 1).astype(F32)
            start_c, stop_c = tab_col[:, 3:4], tab_col[:, 3:4] + tab_col[:, 0:1]
            key_member = (tab_col[:, 2:3] == rank) & (key_row >= start_c) & (key_row < stop_c)
            seg_k = jnp.sum(jnp.where(key_member, key_label, 0.0), axis=0, keepdims=True)
            filled = seg_q > 0.0
            q_pos = lax.broadcasted_iota(jnp.int32, (64, D), 0) + 64
            k_pos = lax.broadcasted_iota(jnp.int32, (64, D), 1)
            own = (seg_q == seg_k) & filled & (k_pos <= q_pos)
            take_first = filled & (owner_q == first)
            take_last = filled & (owner_q == last) & (first != last)
            bias_s[r, :, 0:256] = jnp.broadcast_to(jnp.where(take_first, 0.0, MASKED), (64, PROMPT))
            bias_s[r, :, 256:512] = jnp.broadcast_to(jnp.where(take_last, 0.0, MASKED), (64, PROMPT))
            bias_s[r, :, 512:640] = jnp.where(own, 0.0, MASKED)
            filled_s[r] = jnp.broadcast_to(jnp.where(filled, 1.0, 0.0), (64, D))
            return 0

        lax.fori_loop(0, 4, one, 0)

    def prompts_of(r):
        rank = ((y * 4 + lax.rem(z, 4)) * 4 + r).astype(F32)
        table = tab_s[0:4, :].astype(F32)
        holding = table[2:3, :] == rank
        owner = table[1:2, :]
        first = jnp.min(jnp.where(holding, owner, 15.0))
        last = jnp.max(jnp.where(holding, owner, 0.0))
        return jnp.clip(first.astype(jnp.int32), 0, 15), jnp.clip(last.astype(jnp.int32), 0, 15)

    def stack(parts):
        return jnp.concatenate(parts, axis=0)

    def prompt_rows(p):
        kv = g_in[p].reshape(32, 16, D).astype(F32)
        return kv[:, 0:8, :].reshape(PROMPT, D).astype(BF), kv[:, 8:16, :].reshape(PROMPT, D).astype(BF)

    def keep(n, dk, dv):
        part[n, :, 0:8, :] = dk.reshape(32, 8, D)
        part[n, :, 8:16, :] = dv.reshape(32, 8, D)

    def lead_grads():
        p, zh = y * 4 + lax.rem(z, 4), z // 4
        lead = pqd[...].astype(F32)
        q = stack([lead[:, i * 8 : i * 8 + 8, :].reshape(64, D) for i in range(QPK)]).astype(BF)
        do = stack([lead[:, (i + 5) * 8 : (i + 5) * 8 + 8, :].reshape(64, D) for i in range(QPK)]).astype(BF)
        dls = [dl[j].T for j in range(8)]
        delta = stack([dls[j][32:40, i : i + 1] for i in range(QPK) for j in range(8)])

        def place_of(n, hi):
            j, i = (n // 8) % 8, n % 8
            return (j // 2) * 64 + (hi * 2 + j % 2) * 8 + i

        n_q = lax.broadcasted_iota(jnp.int32, (64, PROMPT), 0)
        n_k = lax.broadcasted_iota(jnp.int32, (64, PROMPT), 1)
        bias = jnp.where(place_of(n_k, n_k // 64) <= place_of(n_q, zh), 0.0, MASKED)
        k, v = prompt_rows(p)
        dq, dk, dv = grads(q, do, delta, k, v, stack([bias] * QPK), True)
        keep(8, dk, dv)
        for j in range(8):
            tiles = [dq[i * 64 + j * 8 : i * 64 + j * 8 + 8] for i in range(QPK)]
            pdq[j] = stack([*tiles, jnp.zeros((8, D), F32)]).astype(BF)

    def cols(ref, h, width):
        return ref.at[:, pl.ds(pl.multiple_of(h * width, D), width)]

    mine = (y * 4 + lax.rem(z, 4), z // 4)
    sources = [
        lambda h: pkv_s.at[h],
        lambda h: cols(rk, h, D),
        lambda h: cols(rv, h, D),
        lambda h: pqd_s.at[h],
        lambda h: cols(rq, h, W),
        lambda h: cols(rdo, h, W),
        lambda h: dl_s.at[h],
    ]
    landing = [
        lambda j: g_in.at[mine[0], mine[1], j],
        lambda j: rkv.at[0, j],
        lambda j: rkv.at[1, j],
        lambda j: pqd.at[j],
        lambda j: rq_in.at[j],
        lambda j: rdo_in.at[j],
        lambda j: dl.at[j],
    ]
    kinds = len(sources)
    own = [pltpu.make_async_copy(sources[n](s), landing[n](s), own_sem.at[n]) for n in range(kinds)]
    sent = []

    def send(n):
        own[n].start()
        for d in range(7):
            h = me.group[d]
            copy = remote(sources[n](h), landing[n](s), a_send.at[n, d], a_recv.at[n, s], me.group_dev[d])
            copy.start()
            sent.append(copy)

    def arrived(n):
        own[n].wait()
        for d in range(7):
            j = me.sender[d]
            remote(landing[n](j), landing[n](j), a_send.at[n, d], a_recv.at[n, j], me.group_dev[d]).wait_recv()

    send(0)
    send(1)
    send(2)
    send(4)
    send(5)
    loads[2].wait()
    loads[3].wait()
    for g in range(8):
        parts = [pq_s[:, (g * QPK + i) * D : (g * QPK + i + 1) * D].astype(F32) for i in range(QPK)]
        parts += [pdo_s[:, (g * QPK + i) * D : (g * QPK + i + 1) * D].astype(F32) for i in range(QPK)]
        pqd_s[g] = jnp.concatenate(parts, axis=0).astype(BF)
    send(3)

    def block(yy, zz):
        return g_in.at[yy * 4 + lax.rem(zz, 4), zz // 4]

    def at(k, m):
        return wrap(z + STEP[k] + NEAR[m], 16)

    def across(k, m):
        there = block(y, at(k, m))
        for d in range(3):
            copy = remote(there, there, y_send.at[4 * k + m, d], y_recv.at[4 * k + m, d], me.y_dev[d])
            copy.start()
            sent.append(copy)

    def along(k, m):
        there = block(y, at(k, 0))
        return remote(there, there, n_send.at[k, m - 1], n_recv.at[k, m - 1], me.z_dev(-NEAR[m]))

    def far(k):
        there = block(y, z)
        return remote(there, there, f_send.at[k - 1], f_recv.at[k - 1], me.z_dev(-STEP[k]))

    def spread(k):
        if k > 0:
            there = block(y, at(k, 0))
            remote(there, there, f_send.at[k - 1], f_recv.at[k - 1], me.up).wait_recv()
        for m in (1, 2, 3):
            copy = along(k, m)
            copy.start()
            sent.append(copy)
        across(k, 0)

    def pass_on(k):
        for m in (1, 2, 3):
            there = block(y, at(k, m))
            remote(there, there, n_send.at[k, m - 1], n_recv.at[k, m - 1], me.up).wait_recv()
            across(k, m)

    arrived(0)
    for k in (3, 1, 2):
        copy = far(k)
        copy.start()
        sent.append(copy)
    spread(0)
    for load in loads[4:]:
        load.wait()
    sums = [head_sums(ro_s, rdo_s, 32), head_sums(po_s, pdo_s, 8), jnp.zeros((D - 40, D), F32)]
    sums = jnp.concatenate(sums, axis=0).T
    for g in range(8):
        dl_s[g, 0:QPK, :] = sums[g * QPK : (g + 1) * QPK, :]
        dl_s[g, QPK:8, :] = jnp.zeros((8 - QPK, D), F32)
    send(6)
    masks()
    pass_on(0)
    arrived(1)
    arrived(2)
    shift = remote(rkv, prev, sh_send, sh_recv, me.up4)
    shift.start()
    spread(1)
    spread(2)
    pass_on(1)
    pass_on(2)
    spread(3)
    pass_on(3)
    for n in range(3, kinds):
        arrived(n)
    lead_grads()
    shift.wait()
    for k in range(4):
        for m in range(4):
            for d in range(3):
                there = block(wrap(y - d - 1, 4), at(k, m))
                remote(there, there, y_send.at[4 * k + m, d], y_recv.at[4 * k + m, d], me.y_dev[d]).wait_recv()


    def rank_grads(r, _):
        first, last = prompts_of(r)
        bias = stack([bias_s[r]] * QPK)
        filled = stack([filled_s[r, :, 0:1]] * QPK) > 0.0
        two = pl.ds(2 * r, 2)
        q2 = rq_in[two].reshape(64, W)
        do2 = rdo_in[two].reshape(64, W)
        q = stack([q2[:, i * D : (i + 1) * D] for i in range(QPK)])
        do = stack([do2[:, i * D : (i + 1) * D] for i in range(QPK)])
        dl2 = dl[two]
        dl0, dl1 = dl2[0].T, dl2[1].T
        delta = stack([half[0:32, i : i + 1] for i in range(QPK) for half in (dl0, dl1)])
        k1, v1 = prompt_rows(first)
        k2, v2 = prompt_rows(last)
        k = stack([k1, k2, prev[0, two].reshape(64, D), rkv[0, two].reshape(64, D)])
        v = stack([v1, v2, prev[1, two].reshape(64, D), rkv[1, two].reshape(64, D)])
        dq, dk, dv = grads(q, do, delta, k, v, bias, filled)
        dq = dq.astype(BF)
        dq_s[two] = jnp.concatenate([dq[i * 64 : (i + 1) * 64] for i in range(QPK)], axis=1).reshape(2, 32, W)
        keep(2 * r, dk[0:256], dv[0:256])
        keep(2 * r + 1, dk[256:512], dv[256:512])
        prev_d[0, two] = dk[512:576].astype(BF).reshape(2, 32, D)
        prev_d[1, two] = dv[512:576].astype(BF).reshape(2, 32, D)
        cur[0, two] = dk[576:640].reshape(2, 32, D)
        cur[1, two] = dv[576:640].reshape(2, 32, D)
        return 0

    lax.fori_loop(0, 4, rank_grads, 0)

    owners = [prompts_of(jnp.int32(r)) for r in range(4)]
    part[9] = jnp.zeros((32, 16, D), F32)

    def summed(yy, zz):
        p, rows = yy * 4 + lax.rem(zz, 4), pl.ds(zz // 4 * 8, 8)
        total = None
        for r, (first, last) in enumerate(owners):
            n = jnp.where(first == p, 2 * r, jnp.where(last == p, 2 * r + 1, 9))
            total = part[n, rows] if total is None else total + part[n, rows]
        return total

    def y_copy(k, m, d):
        n = 4 * k + m
        return remote(y_out.at[d, n], y_in.at[d, n], yo_send.at[n, d], yo_recv.at[n, d], me.y_dev[d])

    def exchange(k):
        for m in (1, 2, 3, 0):
            for d in range(3):
                y_out[d, 4 * k + m] = summed(wrap(y + d + 1, 4), at(k, m)).astype(BF)
                copy = y_copy(k, m, d)
                copy.start()
                sent.append(copy)

    exchange(3)
    shift_back = remote(prev_d, back, sho_send, sho_recv, me.down4)
    shift_back.start()
    exchange(1)
    exchange(2)
    exchange(0)

    out_sources = [
        lambda h: dq_s.at[h],
        lambda h: pdq.at[h],
        lambda h: kv_s.at[0, h],
        lambda h: kv_s.at[1, h],
        lambda h: pkvo_s.at[h],
    ]
    out_landing = [
        lambda j: cols(dq_o, j, W),
        lambda j: pdq_in.at[j],
        lambda j: cols(dk_o, j, D),
        lambda j: cols(dv_o, j, D),
        lambda j: pkv_in.at[j],
    ]
    out_own = {}

    def give(n):
        out_own[n] = pltpu.make_async_copy(out_sources[n](s), out_landing[n](s), owno_sem.at[n])
        out_own[n].start()
        for d in range(7):
            h = me.group[d]
            copy = remote(out_sources[n](h), out_landing[n](s), ao_send.at[n, d], ao_recv.at[n, s], me.group_dev[d])
            copy.start()
            sent.append(copy)

    def taken(n):
        out_own[n].wait()
        for d in range(7):
            j = me.sender[d]
            remote(out_landing[n](j), out_landing[n](j), ao_send.at[n, d], ao_recv.at[n, j], me.group_dev[d]).wait_recv()

    give(0)
    give(1)

    def partial(k, m):
        total = summed(y, at(k, m))
        if m == 0:
            total += part[8, pl.ds(at(k, m) // 4 * 8, 8)]
        for d in range(3):
            y_copy(k, m, d).wait_recv()
            total += y_in[d, 4 * k + m].astype(F32)
        return total

    def n_copy(k, m):
        n = (k, m - 1)
        return remote(n_out.at[*n], n_in.at[*n], no_send.at[*n], no_recv.at[*n], me.z_dev(NEAR[m]))

    def f_copy(k):
        n = k - 1
        return remote(f_out.at[n], f_in.at[n], fo_send.at[n], fo_recv.at[n], me.z_dev(STEP[k]))

    def collect(k):
        for m in (1, 2, 3):
            n_out[k, m - 1] = partial(k, m).astype(BF)
            copy = n_copy(k, m)
            copy.start()
            sent.append(copy)
        own_sum[k] = partial(k, 0)

    def finish(k):
        total = own_sum[k]
        for m in (1, 2, 3):
            n_copy(k, m).wait_recv()
            total += n_in[k, m - 1].astype(F32)
        if k > 0:
            f_out[k - 1] = total.astype(BF)
            copy = f_copy(k)
            copy.start()
            sent.append(copy)
        return total

    collect(3)
    collect(1)
    finish(3)
    collect(2)
    finish(1)
    shift_back.wait_recv()
    kv_s[...] = (cur[...] + back[...].astype(F32)).astype(BF)
    give(2)
    give(3)
    collect(0)
    finish(2)
    total = finish(0)
    for k in (1, 2, 3):
        f_copy(k).wait_recv()
        total += f_in[k - 1].astype(F32)
    pkvo_s[...] = total.astype(BF)
    give(4)
    for n in (1, 0, 2, 3, 4):
        taken(n)
    shift_back.wait_send()
    for copy in sent:
        copy.wait_send()


def finish_kernel(dq, dk, dv, pdq, pkv, dq_o, dk_o, dv_o, pdq_o, pdk_o, pdv_o):
    dq_o[...] = dq[...]
    dk_o[...] = dk[...]
    dv_o[...] = dv[...]
    for h in range(8):
        tiles = pdq[h].astype(F32)
        for i in range(QPK):
            pdq_o[:, (h * QPK + i) * D : (h * QPK + i + 1) * D] = tiles[i * 8 : i * 8 + 8].astype(BF)
        tile = pkv[h].astype(F32)
        pdk_o[:, h * D : (h + 1) * D] = tile[0:8].astype(BF)
        pdv_o[:, h * D : (h + 1) * D] = tile[8:16].astype(BF)


def vmem(n):
    return [pl.BlockSpec(memory_space=pltpu.VMEM)] * n


def shapes(*items):
    return [jax.ShapeDtypeStruct(shape, dtype) for shape, dtype in items]


def local(*args):
    dma = pltpu.SemaphoreType.DMA
    rows, tables = args[:10], [table.reshape(1, 256) for table in args[10:]]
    bf = lambda *shape: pltpu.VMEM(shape, BF)
    f32 = lambda *shape: pltpu.VMEM(shape, F32)
    landed = pl.pallas_call(
        main_kernel,
        out_shape=shapes(
            ((32, 40 * D), BF), ((32, 8 * D), BF), ((32, 8 * D), BF), ((8, 48, D), BF), ((8, 16, D), BF)
        ),
        in_specs=[pl.BlockSpec(memory_space=pl.ANY)] * 14,
        out_specs=vmem(5),
        scratch_shapes=[
            bf(32, 40 * D), bf(32, 40 * D), bf(8, 40 * D), bf(8, 8 * D), bf(8, 8 * D), bf(8, 40 * D), bf(8, 40 * D),
            pltpu.VMEM((8, 256), jnp.int32), bf(8, 16, D), bf(8, 80, D), f32(8, 8, D),
            bf(8, 32, W), bf(8, 32, W), bf(2, 8, 32, D), bf(2, 8, 32, D), bf(16, 4, 8, 16, D), bf(8, 80, D), f32(8, 8, D),
            f32(4, 64, 640), f32(4, 64, D), f32(10, 32, 16, D), bf(8, 32, W), f32(2, 8, 32, D), bf(2, 8, 32, D), bf(8, 48, D),
            bf(2, 8, 32, D), bf(3, 16, 8, 16, D), bf(3, 16, 8, 16, D), f32(4, 8, 16, D), bf(4, 3, 8, 16, D), bf(4, 3, 8, 16, D),
            bf(3, 8, 16, D), bf(3, 8, 16, D), bf(2, 8, 32, D), bf(8, 16, D),
            dma((11,)), dma((7, 7)), dma((7, 8)), dma((7,)), dma, dma,
            dma((3,)), dma((3,)), dma((4, 3)), dma((4, 3)), dma((16, 3)), dma((16, 3)),
            dma((5, 7)), dma((5, 8)), dma((5,)), dma, dma,
            dma((3,)), dma((3,)), dma((4, 3)), dma((4, 3)), dma((16, 3)), dma((16, 3)),
        ],
        compiler_params=pltpu.CompilerParams(collective_id=0, has_side_effects=True, vmem_limit_bytes=60 * 2**20),
        name="exchange_and_grads",
    )(*rows, *tables)
    return tuple(
        pl.pallas_call(
            finish_kernel,
            out_shape=shapes(
                ((32, 40 * D), BF), ((32, 8 * D), BF), ((32, 8 * D), BF),
                ((8, 40 * D), BF), ((8, 8 * D), BF), ((8, 8 * D), BF),
            ),
            in_specs=vmem(5),
            out_specs=vmem(6),
            name="finish",
        )(*landed)
    )


def solution(mesh):
    rows = P(("dp", "head"), None)
    return jax.shard_map(
        local,
        mesh=mesh,
        in_specs=(rows,) * 10 + (P(),) * 4,
        out_specs=(rows,) * 6,
        check_vma=False,
    )
```

```python
import jax
import jax.numpy as jnp
from jax import lax
from jax.experimental import pallas as pl
from jax.experimental.pallas import tpu as pltpu
from jax.sharding import PartitionSpec as P

D = 128
QPK = 5
W = QPK * D
PROMPT = 256
MASKED = -1e30
SCALE = D**-0.5
STEP = (4, 8, -4, 0)
NEAR = (1, 2, -1, 0)
MESH = pl.DeviceIdType.MESH
BF = jnp.bfloat16
F32 = jnp.float32


def coords():
    dp = lax.axis_index("dp")
    hd = lax.axis_index("head")
    x, zl, y = lax.rem(dp, 4), lax.rem(dp // 4, 4), dp // 16
    zh, c = hd // 2, lax.rem(hd, 2)
    return x, y, zh * 4 + zl, c


def place(x, y, z, c):
    return ((y * 4 + lax.rem(z, 4)) * 4 + x, (z // 4) * 2 + c)


def wrap(a, n):
    return lax.rem(a + 4 * n, n)


def remote(src, dst, send_sem, recv_sem, device):
    return pltpu.make_async_remote_copy(
        src_ref=src,
        dst_ref=dst,
        send_sem=send_sem,
        recv_sem=recv_sem,
        device_id=device,
        device_id_type=MESH,
    )


class Peers:
    def __init__(self):
        self.x, self.y, self.z, self.c = coords()
        self.s = 2 * self.x + self.c
        x, y, z, c, s = self.x, self.y, self.z, self.c, self.s
        self.group = [wrap(s + d, 8) for d in range(1, 8)]
        self.group_dev = [place(g // 2, y, z, lax.rem(g, 2)) for g in self.group]
        self.sender = [wrap(s - d, 8) for d in range(1, 8)]
        self.y_dev = [place(x, wrap(y + d, 4), z, c) for d in range(1, 4)]
        self.z_near = [self.z_dev(k) for k in (1, -1, 2, -2)]

    def z_dev(self, k):
        return place(self.x, self.y, wrap(self.z + k, 16), self.c)

    def signal_all(self):
        barrier = pltpu.get_barrier_semaphore()
        peers = [*self.group_dev, *self.y_dev, *self.z_near]
        for peer in peers:
            pl.semaphore_signal(barrier, inc=1, device_id=peer, device_id_type=MESH)
        return barrier, len(peers)


def head_sums(o_ref, do_ref, rows):
    lane = lax.broadcasted_iota(jnp.int32, (rows, D), 1)
    total = jnp.zeros((rows, D), F32)
    for g in range(8 * QPK):
        cols = slice(g * D, (g + 1) * D)
        one = jnp.sum(o_ref[:, cols].astype(F32) * do_ref[:, cols].astype(F32), axis=1, keepdims=True)
        total = jnp.where(lane == g, one, total)
    return total


def dot_t(a, b):
    return lax.dot_general(a, b, (((1,), (1,)), ((), ())), preferred_element_type=F32)


def dot(a, b):
    return lax.dot_general(a, b, (((1,), (0,)), ((), ())), preferred_element_type=F32)


def t_dot(a, b):
    return lax.dot_general(a, b, (((0,), (0,)), ((), ())), preferred_element_type=F32)


def grads(q, do, delta, k, v, bias, filled):
    scores = dot_t(q, k) * SCALE + bias
    highest = jnp.max(scores, axis=1, keepdims=True)
    e = jnp.exp(scores - highest)
    total = jnp.sum(e, axis=1, keepdims=True)
    likely = e * jnp.where(filled, 1.0 / total, 0.0)
    prob_grad = dot_t(do, v)
    score_grad = (likely * (prob_grad - delta)).astype(BF)
    dq = dot(score_grad, k) * SCALE
    dk = t_dot(score_grad, q) * SCALE
    dv = t_dot(likely.astype(BF), do)
    return dq, dk, dv


def main_kernel(
    rq, rk, rv, ro, rdo, pq, pk, pv, po, pdo, resp_len, resp_prompt, plan_rank, plan_offset,
    dq_o, dk_o, dv_o, pdq_in, pkv_in,
    ro_s, rdo_s, pq_s, pk_s, pv_s, po_s, pdo_s, tab_s, pkv_s, pqd_s, dl_s,
    rq_in, rdo_in, rkv, via, prev, g_in, pqd, dl,
    bias_s, filled_s, part, dq_s, cur, prev_d, pdq,
    back, y_out, y_in, own_sum, n_out, n_in, f_out, f_in, kv_s, pkvo_s,
    load_sem, a_send, a_recv, own_sem, sh_send, sh_recv,
    f_send, f_recv, n_send, n_recv, y_send, y_recv,
    ao_send, ao_recv, owno_sem, sho_send, sho_recv,
    fo_send, fo_recv, no_send, no_recv, yo_send, yo_recv,
):
    me = Peers()
    s, y, z = me.s, me.y, me.z
    barrier, count = me.signal_all()
    pairs = [(pk, pk_s), (pv, pv_s), (pq, pq_s), (pdo, pdo_s), (po, po_s), (ro, ro_s), (rdo, rdo_s)]
    loads = [pltpu.make_async_copy(src, dst, load_sem.at[n]) for n, (src, dst) in enumerate(pairs)]
    for load in loads:
        load.start()
    for n, table in enumerate((resp_len, resp_prompt, plan_rank, plan_offset)):
        loads.append(pltpu.make_async_copy(table, tab_s.at[n : n + 1], load_sem.at[7 + n]))
        loads[-1].start()
    loads[0].wait()
    loads[1].wait()
    for g in range(8):
        k8 = pk_s[:, g * D : (g + 1) * D].astype(F32)
        v8 = pv_s[:, g * D : (g + 1) * D].astype(F32)
        pkv_s[g] = jnp.concatenate([k8, v8], axis=0).astype(BF)
    pl.semaphore_wait(barrier, count)

    def masks():
        zh = z // 4
        tab_s[4:8, :] = jnp.zeros((4, 256), jnp.int32)
        tab_row = tab_s[...].astype(F32)
        tab_col = tab_row.T

        def one(r, _):
            rank = ((y * 4 + lax.rem(z, 4)) * 4 + r).astype(F32)
            base = zh * 64
            holding = tab_row[2:3, :] == rank
            owner = tab_row[1:2, :]
            first = jnp.min(jnp.where(holding, owner, 16.0), axis=1, keepdims=True)
            last = jnp.max(jnp.where(holding, owner, 0.0), axis=1, keepdims=True)
            row = (lax.broadcasted_iota(jnp.int32, (64, PROMPT), 0) + base).astype(F32)
            label = (lax.broadcasted_iota(jnp.int32, (64, PROMPT), 1) + 1).astype(F32)
            start, stop = tab_row[3:4, :], tab_row[3:4, :] + tab_row[0:1, :]
            member = holding & (row >= start) & (row < stop)
            seg_q = jnp.sum(jnp.where(member, label, 0.0), axis=1, keepdims=True)
            owner_q = jnp.sum(jnp.where(member, jnp.broadcast_to(owner, member.shape), 0.0), axis=1, keepdims=True)
            key_row = (lax.broadcasted_iota(jnp.int32, (PROMPT, D), 1) + base - 64).astype(F32)
            key_label = (lax.broadcasted_iota(jnp.int32, (PROMPT, D), 0) + 1).astype(F32)
            start_c, stop_c = tab_col[:, 3:4], tab_col[:, 3:4] + tab_col[:, 0:1]
            key_member = (tab_col[:, 2:3] == rank) & (key_row >= start_c) & (key_row < stop_c)
            seg_k = jnp.sum(jnp.where(key_member, key_label, 0.0), axis=0, keepdims=True)
            filled = seg_q > 0.0
            q_pos = lax.broadcasted_iota(jnp.int32, (64, D), 0) + 64
            k_pos = lax.broadcasted_iota(jnp.int32, (64, D), 1)
            own = (seg_q == seg_k) & filled & (k_pos <= q_pos)
            take_first = filled & (owner_q == first)
            take_last = filled & (owner_q == last) & (first != last)
            bias_s[r, :, 0:256] = jnp.broadcast_to(jnp.where(take_first, 0.0, MASKED), (64, PROMPT))
            bias_s[r, :, 256:512] = jnp.broadcast_to(jnp.where(take_last, 0.0, MASKED), (64, PROMPT))
            bias_s[r, :, 512:640] = jnp.where(own, 0.0, MASKED)
            filled_s[r] = jnp.broadcast_to(jnp.where(filled, 1.0, 0.0), (64, D))
            return 0

        lax.fori_loop(0, 4, one, 0)

    def prompts_of(r):
        rank = ((y * 4 + lax.rem(z, 4)) * 4 + r).astype(F32)
        table = tab_s[0:4, :].astype(F32)
        holding = table[2:3, :] == rank
        owner = table[1:2, :]
        first = jnp.min(jnp.where(holding, owner, 15.0))
        last = jnp.max(jnp.where(holding, owner, 0.0))
        return jnp.clip(first.astype(jnp.int32), 0, 15), jnp.clip(last.astype(jnp.int32), 0, 15)

    def stack(parts):
        return jnp.concatenate(parts, axis=0)

    def prompt_rows(p):
        kv = g_in[p].reshape(32, 16, D).astype(F32)
        return kv[:, 0:8, :].reshape(PROMPT, D).astype(BF), kv[:, 8:16, :].reshape(PROMPT, D).astype(BF)

    def keep(n, dk, dv):
        part[n, :, 0:8, :] = dk.reshape(32, 8, D)
        part[n, :, 8:16, :] = dv.reshape(32, 8, D)

    def lead_grads():
        p, zh = y * 4 + lax.rem(z, 4), z // 4
        lead = pqd[...].astype(F32)
        q = stack([lead[:, i * 8 : i * 8 + 8, :].reshape(64, D) for i in range(QPK)]).astype(BF)
        do = stack([lead[:, (i + 5) * 8 : (i + 5) * 8 + 8, :].reshape(64, D) for i in range(QPK)]).astype(BF)
        dls = [dl[j].T for j in range(8)]
        delta = stack([dls[j][32:40, i : i + 1] for i in range(QPK) for j in range(8)])

        def place_of(n, hi):
            j, i = (n // 8) % 8, n % 8
            return (j // 2) * 64 + (hi * 2 + j % 2) * 8 + i

        n_q = lax.broadcasted_iota(jnp.int32, (64, PROMPT), 0)
        n_k = lax.broadcasted_iota(jnp.int32, (64, PROMPT), 1)
        bias = jnp.where(place_of(n_k, n_k // 64) <= place_of(n_q, zh), 0.0, MASKED)
        k, v = prompt_rows(p)
        dq, dk, dv = grads(q, do, delta, k, v, stack([bias] * QPK), True)
        keep(8, dk, dv)
        for j in range(8):
            tiles = [dq[i * 64 + j * 8 : i * 64 + j * 8 + 8] for i in range(QPK)]
            pdq[j] = stack([*tiles, jnp.zeros((8, D), F32)]).astype(BF)

    def cols(ref, h, width):
        return ref.at[:, pl.ds(pl.multiple_of(h * width, D), width)]

    mine = (y * 4 + lax.rem(z, 4), z // 4)
    sources = [
        lambda h: pkv_s.at[h],
        lambda h: cols(rk, h, D),
        lambda h: cols(rv, h, D),
        lambda h: pqd_s.at[h],
        lambda h: cols(rq, h, W),
        lambda h: cols(rdo, h, W),
        lambda h: dl_s.at[h],
    ]
    landing = [
        lambda j: g_in.at[mine[0], mine[1], j],
        lambda j: rkv.at[0, j],
        lambda j: rkv.at[1, j],
        lambda j: pqd.at[j],
        lambda j: rq_in.at[j],
        lambda j: rdo_in.at[j],
        lambda j: dl.at[j],
    ]
    kinds = len(sources)
    own = [pltpu.make_async_copy(sources[n](s), landing[n](s), own_sem.at[n]) for n in range(kinds)]
    sent = []

    def send(n):
        own[n].start()
        for d in range(7):
            h = me.group[d]
            copy = remote(sources[n](h), landing[n](s), a_send.at[n, d], a_recv.at[n, s], me.group_dev[d])
            copy.start()
            sent.append(copy)

    def arrived(n):
        own[n].wait()
        for d in range(7):
            j = me.sender[d]
            remote(landing[n](j), landing[n](j), a_send.at[n, d], a_recv.at[n, j], me.group_dev[d]).wait_recv()

    send(0)
    send(1)
    send(2)
    send(4)
    send(5)
    loads[2].wait()
    loads[3].wait()
    for g in range(8):
        parts = [pq_s[:, (g * QPK + i) * D : (g * QPK + i + 1) * D].astype(F32) for i in range(QPK)]
        parts += [pdo_s[:, (g * QPK + i) * D : (g * QPK + i + 1) * D].astype(F32) for i in range(QPK)]
        pqd_s[g] = jnp.concatenate(parts, axis=0).astype(BF)
    send(3)

    def block(yy, zz):
        return g_in.at[yy * 4 + lax.rem(zz, 4), zz // 4]

    def moved(k):
        return block(y, wrap(z + k, 16))

    def across(k):
        n = k + 8
        for d in range(3):
            copy = remote(moved(k), moved(k), y_send.at[n, d], y_recv.at[n, d], me.y_dev[d])
            copy.start()

    def two(t, sign):
        n = t if sign > 0 else 4 + t
        return remote(moved(-2 * sign * t), moved(-2 * sign * t), f_send.at[n], f_recv.at[n], me.z_dev(2 * sign))

    def one(t, sign):
        n = t if sign > 0 else 4 + t
        return remote(moved(-2 * sign * t), moved(-2 * sign * t), n_send.at[n], n_recv.at[n], me.z_dev(sign))

    def came(copy):
        copy.wait_recv()

    def go(copy):
        copy.start()
        sent.append(copy)

    arrived(0)
    go(two(0, 1))
    go(two(0, -1))
    go(one(0, 1))
    go(one(0, -1))
    across(0)
    for load in loads[4:]:
        load.wait()
    sums = [head_sums(ro_s, rdo_s, 32), head_sums(po_s, pdo_s, 8), jnp.zeros((D - 40, D), F32)]
    sums = jnp.concatenate(sums, axis=0).T
    for g in range(8):
        dl_s[g, 0:QPK, :] = sums[g * QPK : (g + 1) * QPK, :]
        dl_s[g, QPK:8, :] = jnp.zeros((8 - QPK, D), F32)
    send(6)
    masks()
    for t in range(5):
        if t > 0:
            came(two(t - 1, 1))
            if t < 4:
                go(two(t, 1))
                go(one(t, 1))
                came(two(t - 1, -1))
                if t < 3:
                    go(two(t, -1))
                go(one(t, -1))
                across(2 * t)
            across(-2 * t)
        if t == 1:
            arrived(1)
            arrived(2)
            shift = remote(rkv, via, sh_send.at[0], sh_recv.at[0], me.z_dev(2))
            go(shift)
        if t < 4:
            came(one(t, -1))
            across(1 + 2 * t)
            came(one(t, 1))
            across(-1 - 2 * t)
        if t == 3:
            shift.wait_recv()
            shift = remote(via, prev, sh_send.at[1], sh_recv.at[1], me.z_dev(2))
            go(shift)
    for n in range(3, kinds):
        arrived(n)
    lead_grads()
    shift.wait_recv()

    def settle(n, _):
        for d in range(3):
            there = block(wrap(y - d - 1, 4), wrap(z + n - 8, 16))
            remote(there, there, y_send.at[n, d], y_recv.at[n, d], me.y_dev[d]).wait_recv()
            remote(moved(0), moved(0), y_send.at[n, d], y_recv.at[n, d], me.y_dev[d]).wait_send()
        return 0

    lax.fori_loop(0, 16, settle, 0)

    def rank_grads(r, _):
        first, last = prompts_of(r)
        bias = stack([bias_s[r]] * QPK)
        filled = stack([filled_s[r, :, 0:1]] * QPK) > 0.0
        two = pl.ds(2 * r, 2)
        q2 = rq_in[two].reshape(64, W)
        do2 = rdo_in[two].reshape(64, W)
        q = stack([q2[:, i * D : (i + 1) * D] for i in range(QPK)])
        do = stack([do2[:, i * D : (i + 1) * D] for i in range(QPK)])
        dl2 = dl[two]
        dl0, dl1 = dl2[0].T, dl2[1].T
        delta = stack([half[0:32, i : i + 1] for i in range(QPK) for half in (dl0, dl1)])
        k1, v1 = prompt_rows(first)
        k2, v2 = prompt_rows(last)
        k = stack([k1, k2, prev[0, two].reshape(64, D), rkv[0, two].reshape(64, D)])
        v = stack([v1, v2, prev[1, two].reshape(64, D), rkv[1, two].reshape(64, D)])
        dq, dk, dv = grads(q, do, delta, k, v, bias, filled)
        dq = dq.astype(BF)
        dq_s[two] = jnp.concatenate([dq[i * 64 : (i + 1) * 64] for i in range(QPK)], axis=1).reshape(2, 32, W)
        keep(2 * r, dk[0:256], dv[0:256])
        keep(2 * r + 1, dk[256:512], dv[256:512])
        prev_d[0, two] = dk[512:576].astype(BF).reshape(2, 32, D)
        prev_d[1, two] = dv[512:576].astype(BF).reshape(2, 32, D)
        cur[0, two] = dk[576:640].reshape(2, 32, D)
        cur[1, two] = dv[576:640].reshape(2, 32, D)
        return 0

    lax.fori_loop(0, 4, rank_grads, 0)

    owners = [prompts_of(jnp.int32(r)) for r in range(4)]
    part[9] = jnp.zeros((32, 16, D), F32)

    def summed(yy, zz):
        p, rows = yy * 4 + lax.rem(zz, 4), pl.ds(zz // 4 * 8, 8)
        total = None
        for r, (first, last) in enumerate(owners):
            n = jnp.where(first == p, 2 * r, jnp.where(last == p, 2 * r + 1, 9))
            total = part[n, rows] if total is None else total + part[n, rows]
        return total

    def at(k, m):
        return wrap(z + STEP[k] + NEAR[m], 16)

    def y_copy(n, d):
        return remote(y_out.at[d, n], y_in.at[d, n], yo_send.at[n, d], yo_recv.at[n, d], me.y_dev[d])

    def exchange(n, _):
        m = lax.rem(n, 4) + 1
        zz = wrap(z + 4 * (n // 4 + 1) + m - 4 * (m // 3), 16)
        for d in range(3):
            y_out[d, n] = summed(wrap(y + d + 1, 4), zz).astype(BF)
            y_copy(n, d).start()
        return 0

    lax.fori_loop(0, 4, exchange, 0)
    shift_back = remote(prev_d, back, sho_send, sho_recv, me.z_dev(-4))
    shift_back.start()
    lax.fori_loop(4, 16, exchange, 0)

    out_sources = [
        lambda h: dq_s.at[h],
        lambda h: pdq.at[h],
        lambda h: kv_s.at[0, h],
        lambda h: kv_s.at[1, h],
        lambda h: pkvo_s.at[h],
    ]
    out_landing = [
        lambda j: cols(dq_o, j, W),
        lambda j: pdq_in.at[j],
        lambda j: cols(dk_o, j, D),
        lambda j: cols(dv_o, j, D),
        lambda j: pkv_in.at[j],
    ]
    out_own = {}

    def give(n):
        out_own[n] = pltpu.make_async_copy(out_sources[n](s), out_landing[n](s), owno_sem.at[n])
        out_own[n].start()
        for d in range(7):
            h = me.group[d]
            copy = remote(out_sources[n](h), out_landing[n](s), ao_send.at[n, d], ao_recv.at[n, s], me.group_dev[d])
            copy.start()
            sent.append(copy)

    def taken(n):
        out_own[n].wait()
        for d in range(7):
            j = me.sender[d]
            remote(out_landing[n](j), out_landing[n](j), ao_send.at[n, d], ao_recv.at[n, j], me.group_dev[d]).wait_recv()

    give(0)
    give(1)

    def partial(k, m):
        total = summed(y, at(k, m))
        if m == 3:
            total += part[8, pl.ds(at(k, m) // 4 * 8, 8)]
        for d in range(3):
            y_copy(4 * k + m, d).wait_recv()
            total += y_in[d, 4 * k + m].astype(F32)
        return total

    def n_copy(k, m):
        return remote(n_out.at[k, m], n_in.at[k, m], no_send.at[k, m], no_recv.at[k, m], me.z_dev(NEAR[m]))

    def f_copy(k):
        return remote(f_out.at[k], f_in.at[k], fo_send.at[k], fo_recv.at[k], me.z_dev(STEP[k]))

    def collect(k):
        for m in range(3):
            n_out[k, m] = partial(k, m).astype(BF)
            go(n_copy(k, m))
        own_sum[k] = partial(k, 3)

    def finish(k):
        total = own_sum[k]
        for m in range(3):
            came(n_copy(k, m))
            total += n_in[k, m].astype(F32)
        if k < 3:
            f_out[k] = total.astype(BF)
            go(f_copy(k))
        return total

    collect(0)
    collect(1)
    finish(0)
    collect(2)
    finish(1)
    shift_back.wait_recv()
    kv_s[...] = (cur[...] + back[...].astype(F32)).astype(BF)
    give(2)
    give(3)
    collect(3)
    finish(2)
    total = finish(3)
    for k in range(3):
        came(f_copy(k))
        total += f_in[k].astype(F32)
    pkvo_s[...] = total.astype(BF)
    give(4)
    for n in (1, 0, 2, 3, 4):
        taken(n)
    shift_back.wait_send()
    for copy in sent:
        copy.wait_send()

    def leave(n, _):
        for d in range(3):
            y_copy(n, d).wait_send()
        return 0

    lax.fori_loop(0, 16, leave, 0)


def finish_kernel(dq, dk, dv, pdq, pkv, dq_o, dk_o, dv_o, pdq_o, pdk_o, pdv_o):
    dq_o[...] = dq[...]
    dk_o[...] = dk[...]
    dv_o[...] = dv[...]
    for h in range(8):
        tiles = pdq[h].astype(F32)
        for i in range(QPK):
            pdq_o[:, (h * QPK + i) * D : (h * QPK + i + 1) * D] = tiles[i * 8 : i * 8 + 8].astype(BF)
        tile = pkv[h].astype(F32)
        pdk_o[:, h * D : (h + 1) * D] = tile[0:8].astype(BF)
        pdv_o[:, h * D : (h + 1) * D] = tile[8:16].astype(BF)


def vmem(n):
    return [pl.BlockSpec(memory_space=pltpu.VMEM)] * n


def shapes(*items):
    return [jax.ShapeDtypeStruct(shape, dtype) for shape, dtype in items]


def local(*args):
    dma = pltpu.SemaphoreType.DMA
    rows, tables = args[:10], [table.reshape(1, 256) for table in args[10:]]
    bf = lambda *shape: pltpu.VMEM(shape, BF)
    f32 = lambda *shape: pltpu.VMEM(shape, F32)
    landed = pl.pallas_call(
        main_kernel,
        out_shape=shapes(
            ((32, 40 * D), BF), ((32, 8 * D), BF), ((32, 8 * D), BF), ((8, 48, D), BF), ((8, 16, D), BF)
        ),
        in_specs=[pl.BlockSpec(memory_space=pl.ANY)] * 14,
        out_specs=vmem(5),
        scratch_shapes=[
            bf(32, 40 * D), bf(32, 40 * D), bf(8, 40 * D), bf(8, 8 * D), bf(8, 8 * D), bf(8, 40 * D), bf(8, 40 * D),
            pltpu.VMEM((8, 256), jnp.int32), bf(8, 16, D), bf(8, 80, D), f32(8, 8, D),
            bf(8, 32, W), bf(8, 32, W), bf(2, 8, 32, D), bf(2, 8, 32, D), bf(2, 8, 32, D), bf(16, 4, 8, 16, D), bf(8, 80, D), f32(8, 8, D),
            f32(4, 64, 640), f32(4, 64, D), f32(10, 32, 16, D), bf(8, 32, W), f32(2, 8, 32, D), bf(2, 8, 32, D), bf(8, 48, D),
            bf(2, 8, 32, D), bf(3, 16, 8, 16, D), bf(3, 16, 8, 16, D), f32(4, 8, 16, D), bf(4, 3, 8, 16, D), bf(4, 3, 8, 16, D),
            bf(3, 8, 16, D), bf(3, 8, 16, D), bf(2, 8, 32, D), bf(8, 16, D),
            dma((11,)), dma((7, 7)), dma((7, 8)), dma((7,)), dma((2,)), dma((2,)),
            dma((7,)), dma((7,)), dma((8,)), dma((8,)), dma((16, 3)), dma((16, 3)),
            dma((5, 7)), dma((5, 8)), dma((5,)), dma, dma,
            dma((3,)), dma((3,)), dma((4, 3)), dma((4, 3)), dma((16, 3)), dma((16, 3)),
        ],
        compiler_params=pltpu.CompilerParams(collective_id=0, has_side_effects=True, vmem_limit_bytes=60 * 2**20),
        name="exchange_and_grads",
    )(*rows, *tables)
    return tuple(
        pl.pallas_call(
            finish_kernel,
            out_shape=shapes(
                ((32, 40 * D), BF), ((32, 8 * D), BF), ((32, 8 * D), BF),
                ((8, 40 * D), BF), ((8, 8 * D), BF), ((8, 8 * D), BF),
            ),
            in_specs=vmem(5),
            out_specs=vmem(6),
            name="finish",
        )(*landed)
    )


def solution(mesh):
    rows = P(("dp", "head"), None)
    return jax.shard_map(
        local,
        mesh=mesh,
        in_specs=(rows,) * 10 + (P(),) * 4,
        out_specs=(rows,) * 6,
        check_vma=False,
    )
```

```python
import jax
import jax.numpy as jnp
from jax import lax
from jax.experimental import pallas as pl
from jax.experimental.pallas import tpu as pltpu
from jax.sharding import PartitionSpec as P

D = 128
QPK = 5
W = QPK * D
PROMPT = 256
MASKED = -1e30
SCALE = D**-0.5
STEP = (4, 8, -4, 0)
NEAR = (1, 2, -1, 0)
MESH = pl.DeviceIdType.MESH
BF = jnp.bfloat16
F32 = jnp.float32


def coords():
    dp = lax.axis_index("dp")
    hd = lax.axis_index("head")
    x, zl, y = lax.rem(dp, 4), lax.rem(lax.div(dp, 4), 4), lax.div(dp, 16)
    zh, c = lax.div(hd, 2), lax.rem(hd, 2)
    return x, y, zh * 4 + zl, c


def place(x, y, z, c):
    return ((y * 4 + lax.rem(z, 4)) * 4 + x, lax.div(z, 4) * 2 + c)


def wrap(a, n):
    return lax.rem(a + 4 * n, n)


def remote(src, dst, send_sem, recv_sem, device):
    return pltpu.make_async_remote_copy(
        src_ref=src,
        dst_ref=dst,
        send_sem=send_sem,
        recv_sem=recv_sem,
        device_id=device,
        device_id_type=MESH,
    )


class Peers:
    def __init__(self):
        self.x, self.y, self.z, self.c = coords()
        self.s = 2 * self.x + self.c
        x, y, z, c, s = self.x, self.y, self.z, self.c, self.s
        self.group = [wrap(s + d, 8) for d in range(1, 8)]
        self.group_dev = [place(lax.div(g, 2), y, z, lax.rem(g, 2)) for g in self.group]
        self.sender = [wrap(s - d, 8) for d in range(1, 8)]
        self.y_dev = [place(x, wrap(y + d, 4), z, c) for d in range(1, 4)]
        self.z_near = [self.z_dev(k) for k in (1, -1, 2, -2)]

    def z_dev(self, k):
        return place(self.x, self.y, wrap(self.z + k, 16), self.c)

    def signal_all(self):
        barrier = pltpu.get_barrier_semaphore()
        peers = [*self.group_dev, *self.y_dev, *self.z_near]
        for peer in peers:
            pl.semaphore_signal(barrier, inc=1, device_id=peer, device_id_type=MESH)
        return barrier, len(peers)


def head_sums(o_ref, do_ref, rows):
    lane = lax.broadcasted_iota(jnp.int32, (rows, D), 1)
    total = jnp.zeros((rows, D), F32)
    for g in range(8 * QPK):
        cols = slice(g * D, (g + 1) * D)
        one = jnp.sum(o_ref[:, cols].astype(F32) * do_ref[:, cols].astype(F32), axis=1, keepdims=True)
        total = jnp.where(lane == g, one, total)
    return total


def dot_t(a, b):
    return lax.dot_general(a, b, (((1,), (1,)), ((), ())), preferred_element_type=F32)


def dot(a, b):
    return lax.dot_general(a, b, (((1,), (0,)), ((), ())), preferred_element_type=F32)


def t_dot(a, b):
    return lax.dot_general(a, b, (((0,), (0,)), ((), ())), preferred_element_type=F32)


def grads(q, do, delta, k, v, bias, filled):
    scores = dot_t(q, k) * SCALE + bias
    highest = jnp.max(scores, axis=1, keepdims=True)
    e = jnp.exp(scores - highest)
    total = jnp.sum(e, axis=1, keepdims=True)
    likely = e * jnp.where(filled, 1.0 / total, 0.0)
    prob_grad = dot_t(do, v)
    score_grad = (likely * (prob_grad - delta)).astype(BF)
    dq = dot(score_grad, k) * SCALE
    dk = t_dot(score_grad, q) * SCALE
    dv = t_dot(likely.astype(BF), do)
    return dq, dk, dv


def main_kernel(
    rq, rk, rv, ro, rdo, pq, pk, pv, po, pdo, resp_len, resp_prompt, plan_rank, plan_offset,
    dq_o, dk_o, dv_o, pdq_in, pkv_in,
    ro_s, rdo_s, pq_s, pk_s, pv_s, po_s, pdo_s, tab_s, pkv_s, pqd_s, dl_s,
    rq_in, rdo_in, rkv, via, prev, g_in, pqd, dl,
    bias_s, filled_s, part, dq_s, cur, prev_d, pdq,
    back, y_out, y_in, own_sum, n_out, n_in, f_out, f_in, kv_s, pkvo_s,
    load_sem, a_send, a_recv, own_sem, sh_send, sh_recv,
    f_send, f_recv, n_send, n_recv, y_send, y_recv,
    ao_send, ao_recv, owno_sem, sho_send, sho_recv,
    fo_send, fo_recv, no_send, no_recv, yo_send, yo_recv,
):
    me = Peers()
    s, y, z = me.s, me.y, me.z
    barrier, count = me.signal_all()
    pairs = [(pk, pk_s), (pv, pv_s), (pq, pq_s), (pdo, pdo_s), (po, po_s), (ro, ro_s), (rdo, rdo_s)]
    loads = [pltpu.make_async_copy(src, dst, load_sem.at[n]) for n, (src, dst) in enumerate(pairs)]
    for load in loads:
        load.start()
    for n, table in enumerate((resp_len, resp_prompt, plan_rank, plan_offset)):
        loads.append(pltpu.make_async_copy(table, tab_s.at[n : n + 1], load_sem.at[7 + n]))
        loads[-1].start()
    loads[0].wait()
    loads[1].wait()
    for g in range(8):
        k8 = pk_s[:, g * D : (g + 1) * D].astype(F32)
        v8 = pv_s[:, g * D : (g + 1) * D].astype(F32)
        pkv_s[g] = jnp.concatenate([k8, v8], axis=0).astype(BF)
    pl.semaphore_wait(barrier, count)

    def masks():
        zh = lax.div(z, 4)
        tab_s[4:8, :] = jnp.zeros((4, 256), jnp.int32)
        tab_row = tab_s[...].astype(F32)
        tab_col = tab_row.T

        def one(r, _):
            rank = ((y * 4 + lax.rem(z, 4)) * 4 + r).astype(F32)
            base = zh * 64
            holding = tab_row[2:3, :] == rank
            owner = tab_row[1:2, :]
            first = jnp.min(jnp.where(holding, owner, 16.0), axis=1, keepdims=True)
            last = jnp.max(jnp.where(holding, owner, 0.0), axis=1, keepdims=True)
            row = (lax.broadcasted_iota(jnp.int32, (64, PROMPT), 0) + base).astype(F32)
            label = (lax.broadcasted_iota(jnp.int32, (64, PROMPT), 1) + 1).astype(F32)
            start, stop = tab_row[3:4, :], tab_row[3:4, :] + tab_row[0:1, :]
            member = holding & (row >= start) & (row < stop)
            seg_q = jnp.sum(jnp.where(member, label, 0.0), axis=1, keepdims=True)
            owner_q = jnp.sum(jnp.where(member, jnp.broadcast_to(owner, member.shape), 0.0), axis=1, keepdims=True)
            key_row = (lax.broadcasted_iota(jnp.int32, (PROMPT, D), 1) + base - 64).astype(F32)
            key_label = (lax.broadcasted_iota(jnp.int32, (PROMPT, D), 0) + 1).astype(F32)
            start_c, stop_c = tab_col[:, 3:4], tab_col[:, 3:4] + tab_col[:, 0:1]
            key_member = (tab_col[:, 2:3] == rank) & (key_row >= start_c) & (key_row < stop_c)
            seg_k = jnp.sum(jnp.where(key_member, key_label, 0.0), axis=0, keepdims=True)
            filled = seg_q > 0.0
            q_pos = lax.broadcasted_iota(jnp.int32, (64, D), 0) + 64
            k_pos = lax.broadcasted_iota(jnp.int32, (64, D), 1)
            own = (seg_q == seg_k) & filled & (k_pos <= q_pos)
            take_first = filled & (owner_q == first)
            take_last = filled & (owner_q == last) & (first != last)
            bias_s[r, :, 0:256] = jnp.broadcast_to(jnp.where(take_first, 0.0, MASKED), (64, PROMPT))
            bias_s[r, :, 256:512] = jnp.broadcast_to(jnp.where(take_last, 0.0, MASKED), (64, PROMPT))
            bias_s[r, :, 512:640] = jnp.where(own, 0.0, MASKED)
            filled_s[r] = jnp.broadcast_to(jnp.where(filled, 1.0, 0.0), (64, D))
            return 0

        lax.fori_loop(0, 4, one, 0)

    def prompts_of(r):
        rank = ((y * 4 + lax.rem(z, 4)) * 4 + r).astype(F32)
        table = tab_s[0:4, :].astype(F32)
        holding = table[2:3, :] == rank
        owner = table[1:2, :]
        first = jnp.min(jnp.where(holding, owner, 15.0))
        last = jnp.max(jnp.where(holding, owner, 0.0))
        return jnp.clip(first.astype(jnp.int32), 0, 15), jnp.clip(last.astype(jnp.int32), 0, 15)

    def stack(parts):
        return jnp.concatenate(parts, axis=0)

    def prompt_rows(p):
        kv = g_in[p].reshape(32, 16, D).astype(F32)
        return kv[:, 0:8, :].reshape(PROMPT, D).astype(BF), kv[:, 8:16, :].reshape(PROMPT, D).astype(BF)

    def keep(n, dk, dv):
        part[n, :, 0:8, :] = dk.reshape(32, 8, D)
        part[n, :, 8:16, :] = dv.reshape(32, 8, D)

    def lead_grads():
        p, zh = y * 4 + lax.rem(z, 4), lax.div(z, 4)
        lead = pqd[...].astype(F32)
        q = stack([lead[:, i * 8 : i * 8 + 8, :].reshape(64, D) for i in range(QPK)]).astype(BF)
        do = stack([lead[:, (i + 5) * 8 : (i + 5) * 8 + 8, :].reshape(64, D) for i in range(QPK)]).astype(BF)
        dls = [dl[j].T for j in range(8)]
        delta = stack([dls[j][32:40, i : i + 1] for i in range(QPK) for j in range(8)])

        def place_of(n, hi):
            j, i = (n // 8) % 8, n % 8
            return (j // 2) * 64 + (hi * 2 + j % 2) * 8 + i

        n_q = lax.broadcasted_iota(jnp.int32, (64, PROMPT), 0)
        n_k = lax.broadcasted_iota(jnp.int32, (64, PROMPT), 1)
        bias = jnp.where(place_of(n_k, n_k // 64) <= place_of(n_q, zh), 0.0, MASKED)
        k, v = prompt_rows(p)
        dq, dk, dv = grads(q, do, delta, k, v, stack([bias] * QPK), True)
        keep(8, dk, dv)
        for j in range(8):
            tiles = [dq[i * 64 + j * 8 : i * 64 + j * 8 + 8] for i in range(QPK)]
            pdq[j] = stack([*tiles, jnp.zeros((8, D), F32)]).astype(BF)

    def cols(ref, h, width):
        return ref.at[:, pl.ds(pl.multiple_of(h * width, D), width)]

    mine = (y * 4 + lax.rem(z, 4), lax.div(z, 4))
    sources = [
        lambda h: pkv_s.at[h],
        lambda h: cols(rk, h, D),
        lambda h: cols(rv, h, D),
        lambda h: pqd_s.at[h],
        lambda h: cols(rq, h, W),
        lambda h: cols(rdo, h, W),
        lambda h: dl_s.at[h],
    ]
    landing = [
        lambda j: g_in.at[mine[0], mine[1], j],
        lambda j: rkv.at[0, j],
        lambda j: rkv.at[1, j],
        lambda j: pqd.at[j],
        lambda j: rq_in.at[j],
        lambda j: rdo_in.at[j],
        lambda j: dl.at[j],
    ]
    kinds = len(sources)
    own = [pltpu.make_async_copy(sources[n](s), landing[n](s), own_sem.at[n]) for n in range(kinds)]
    sent = []

    def send(n):
        own[n].start()
        for d in range(7):
            h = me.group[d]
            copy = remote(sources[n](h), landing[n](s), a_send.at[n, d], a_recv.at[n, s], me.group_dev[d])
            copy.start()
            sent.append(copy)

    def arrived(n):
        own[n].wait()
        for d in range(7):
            j = me.sender[d]
            remote(landing[n](j), landing[n](j), a_send.at[n, d], a_recv.at[n, j], me.group_dev[d]).wait_recv()

    send(0)
    send(1)
    send(2)
    send(4)
    send(5)
    loads[2].wait()
    loads[3].wait()
    for g in range(8):
        parts = [pq_s[:, (g * QPK + i) * D : (g * QPK + i + 1) * D].astype(F32) for i in range(QPK)]
        parts += [pdo_s[:, (g * QPK + i) * D : (g * QPK + i + 1) * D].astype(F32) for i in range(QPK)]
        pqd_s[g] = jnp.concatenate(parts, axis=0).astype(BF)
    send(3)

    def block(yy, zz):
        return g_in.at[yy * 4 + lax.rem(zz, 4), lax.div(zz, 4)]

    def moved(k):
        return block(y, wrap(z + k, 16))

    def across(k):
        n = k + 8
        for d in range(3):
            copy = remote(moved(k), moved(k), y_send.at[n, d], y_recv.at[n, d], me.y_dev[d])
            copy.start()

    def two(t, sign):
        n = t if sign > 0 else 4 + t
        return remote(moved(-2 * sign * t), moved(-2 * sign * t), f_send.at[n], f_recv.at[n], me.z_dev(2 * sign))

    def one(t, sign):
        n = t if sign > 0 else 4 + t
        return remote(moved(-2 * sign * t), moved(-2 * sign * t), n_send.at[n], n_recv.at[n], me.z_dev(sign))

    def came(copy):
        copy.wait_recv()

    def go(copy):
        copy.start()
        sent.append(copy)

    arrived(0)
    go(two(0, 1))
    go(two(0, -1))
    go(one(0, 1))
    go(one(0, -1))
    across(0)
    for load in loads[4:]:
        load.wait()
    sums = [head_sums(ro_s, rdo_s, 32), head_sums(po_s, pdo_s, 8), jnp.zeros((D - 40, D), F32)]
    sums = jnp.concatenate(sums, axis=0).T
    for g in range(8):
        dl_s[g, 0:QPK, :] = sums[g * QPK : (g + 1) * QPK, :]
        dl_s[g, QPK:8, :] = jnp.zeros((8 - QPK, D), F32)
    send(6)
    masks()
    for t in range(5):
        if t > 0:
            came(two(t - 1, 1))
            if t < 4:
                go(two(t, 1))
                go(one(t, 1))
                came(two(t - 1, -1))
                if t < 3:
                    go(two(t, -1))
                go(one(t, -1))
                across(2 * t)
            across(-2 * t)
        if t == 1:
            arrived(1)
            arrived(2)
            shift = remote(rkv, via, sh_send.at[0], sh_recv.at[0], me.z_dev(2))
            go(shift)
        if t < 4:
            came(one(t, -1))
            across(1 + 2 * t)
            came(one(t, 1))
            across(-1 - 2 * t)
        if t == 3:
            shift.wait_recv()
            shift = remote(via, prev, sh_send.at[1], sh_recv.at[1], me.z_dev(2))
            go(shift)
    for n in range(3, kinds):
        arrived(n)
    lead_grads()
    shift.wait_recv()

    def settle(n, _):
        for d in range(3):
            there = block(wrap(y - d - 1, 4), wrap(z + n - 8, 16))
            remote(there, there, y_send.at[n, d], y_recv.at[n, d], me.y_dev[d]).wait_recv()
            remote(moved(0), moved(0), y_send.at[n, d], y_recv.at[n, d], me.y_dev[d]).wait_send()
        return 0

    lax.fori_loop(0, 16, settle, 0)

    def rank_grads(r, _):
        first, last = prompts_of(r)
        bias = stack([bias_s[r]] * QPK)
        filled = stack([filled_s[r, :, 0:1]] * QPK) > 0.0
        two = pl.ds(2 * r, 2)
        q2 = rq_in[two].reshape(64, W)
        do2 = rdo_in[two].reshape(64, W)
        q = stack([q2[:, i * D : (i + 1) * D] for i in range(QPK)])
        do = stack([do2[:, i * D : (i + 1) * D] for i in range(QPK)])
        dl2 = dl[two]
        dl0, dl1 = dl2[0].T, dl2[1].T
        delta = stack([half[0:32, i : i + 1] for i in range(QPK) for half in (dl0, dl1)])
        k1, v1 = prompt_rows(first)
        k2, v2 = prompt_rows(last)
        k = stack([k1, k2, prev[0, two].reshape(64, D), rkv[0, two].reshape(64, D)])
        v = stack([v1, v2, prev[1, two].reshape(64, D), rkv[1, two].reshape(64, D)])
        dq, dk, dv = grads(q, do, delta, k, v, bias, filled)
        dq = dq.astype(BF)
        dq_s[two] = jnp.concatenate([dq[i * 64 : (i + 1) * 64] for i in range(QPK)], axis=1).reshape(2, 32, W)
        keep(2 * r, dk[0:256], dv[0:256])
        keep(2 * r + 1, dk[256:512], dv[256:512])
        prev_d[0, two] = dk[512:576].astype(BF).reshape(2, 32, D)
        prev_d[1, two] = dv[512:576].astype(BF).reshape(2, 32, D)
        cur[0, two] = dk[576:640].reshape(2, 32, D)
        cur[1, two] = dv[576:640].reshape(2, 32, D)
        return 0

    def two_ranks(r, _):
        rank_grads(2 * r, 0)
        return rank_grads(2 * r + 1, 0)

    lax.fori_loop(0, 2, two_ranks, 0)

    owners = [prompts_of(jnp.int32(r)) for r in range(4)]
    part[9] = jnp.zeros((32, 16, D), F32)

    def summed(yy, zz):
        p, rows = yy * 4 + lax.rem(zz, 4), pl.ds(lax.div(zz, 4) * 8, 8)
        total = None
        for r, (first, last) in enumerate(owners):
            n = jnp.where(first == p, 2 * r, jnp.where(last == p, 2 * r + 1, 9))
            total = part[n, rows] if total is None else total + part[n, rows]
        return total

    def at(k, m):
        return wrap(z + STEP[k] + NEAR[m], 16)

    def y_copy(n, d):
        return remote(y_out.at[d, n], y_in.at[d, n], yo_send.at[n, d], yo_recv.at[n, d], me.y_dev[d])

    def exchange(n, _):
        m = lax.rem(n, 4) + 1
        zz = wrap(z + 4 * (lax.div(n, 4) + 1) + m - 4 * lax.div(m, 3), 16)
        for d in range(3):
            y_out[d, n] = summed(wrap(y + d + 1, 4), zz).astype(BF)
            y_copy(n, d).start()
        return 0

    lax.fori_loop(0, 4, exchange, 0)
    shift_back = remote(prev_d, back, sho_send, sho_recv, me.z_dev(-4))
    shift_back.start()
    lax.fori_loop(4, 16, exchange, 0)

    out_sources = [
        lambda h: dq_s.at[h],
        lambda h: pdq.at[h],
        lambda h: kv_s.at[0, h],
        lambda h: kv_s.at[1, h],
        lambda h: pkvo_s.at[h],
    ]
    out_landing = [
        lambda j: cols(dq_o, j, W),
        lambda j: pdq_in.at[j],
        lambda j: cols(dk_o, j, D),
        lambda j: cols(dv_o, j, D),
        lambda j: pkv_in.at[j],
    ]
    out_own = {}

    def give(n):
        out_own[n] = pltpu.make_async_copy(out_sources[n](s), out_landing[n](s), owno_sem.at[n])
        out_own[n].start()
        for d in range(7):
            h = me.group[d]
            copy = remote(out_sources[n](h), out_landing[n](s), ao_send.at[n, d], ao_recv.at[n, s], me.group_dev[d])
            copy.start()
            sent.append(copy)

    def taken(n):
        out_own[n].wait()
        for d in range(7):
            j = me.sender[d]
            remote(out_landing[n](j), out_landing[n](j), ao_send.at[n, d], ao_recv.at[n, j], me.group_dev[d]).wait_recv()

    give(0)
    give(1)

    def partial(k, m):
        total = summed(y, at(k, m))
        if m == 3:
            total += part[8, pl.ds(lax.div(at(k, m), 4) * 8, 8)]
        for d in range(3):
            y_copy(4 * k + m, d).wait_recv()
            total += y_in[d, 4 * k + m].astype(F32)
        return total

    def n_copy(k, m):
        return remote(n_out.at[k, m], n_in.at[k, m], no_send.at[k, m], no_recv.at[k, m], me.z_dev(NEAR[m]))

    def f_copy(k):
        return remote(f_out.at[k], f_in.at[k], fo_send.at[k], fo_recv.at[k], me.z_dev(STEP[k]))

    def collect(k):
        for m in range(3):
            n_out[k, m] = partial(k, m).astype(BF)
            go(n_copy(k, m))
        own_sum[k] = partial(k, 3)

    def finish(k):
        total = own_sum[k]
        for m in range(3):
            came(n_copy(k, m))
            total += n_in[k, m].astype(F32)
        if k < 3:
            f_out[k] = total.astype(BF)
            go(f_copy(k))
        return total

    collect(0)
    collect(1)
    finish(0)
    collect(2)
    finish(1)
    shift_back.wait_recv()
    kv_s[...] = (cur[...] + back[...].astype(F32)).astype(BF)
    give(2)
    give(3)
    collect(3)
    finish(2)
    total = finish(3)
    for k in range(3):
        came(f_copy(k))
        total += f_in[k].astype(F32)
    pkvo_s[...] = total.astype(BF)
    give(4)
    for n in (1, 0, 2, 3, 4):
        taken(n)
    shift_back.wait_send()
    for copy in sent:
        copy.wait_send()

    def leave(n, _):
        for d in range(3):
            y_copy(n, d).wait_send()
        return 0

    lax.fori_loop(0, 16, leave, 0)


def finish_kernel(dq, dk, dv, pdq, pkv, dq_o, dk_o, dv_o, pdq_o, pdk_o, pdv_o):
    dq_o[...] = dq[...]
    dk_o[...] = dk[...]
    dv_o[...] = dv[...]
    for h in range(8):
        tiles = pdq[h].astype(F32)
        for i in range(QPK):
            pdq_o[:, (h * QPK + i) * D : (h * QPK + i + 1) * D] = tiles[i * 8 : i * 8 + 8].astype(BF)
        tile = pkv[h].astype(F32)
        pdk_o[:, h * D : (h + 1) * D] = tile[0:8].astype(BF)
        pdv_o[:, h * D : (h + 1) * D] = tile[8:16].astype(BF)


def vmem(n):
    return [pl.BlockSpec(memory_space=pltpu.VMEM)] * n


def shapes(*items):
    return [jax.ShapeDtypeStruct(shape, dtype) for shape, dtype in items]


def local(*args):
    dma = pltpu.SemaphoreType.DMA
    rows, tables = args[:10], [table.reshape(1, 256) for table in args[10:]]
    bf = lambda *shape: pltpu.VMEM(shape, BF)
    f32 = lambda *shape: pltpu.VMEM(shape, F32)
    landed = pl.pallas_call(
        main_kernel,
        out_shape=shapes(
            ((32, 40 * D), BF), ((32, 8 * D), BF), ((32, 8 * D), BF), ((8, 48, D), BF), ((8, 16, D), BF)
        ),
        in_specs=[pl.BlockSpec(memory_space=pl.ANY)] * 14,
        out_specs=[pl.BlockSpec(memory_space=pl.ANY)] * 5,
        scratch_shapes=[
            bf(32, 40 * D), bf(32, 40 * D), bf(8, 40 * D), bf(8, 8 * D), bf(8, 8 * D), bf(8, 40 * D), bf(8, 40 * D),
            pltpu.VMEM((8, 256), jnp.int32), bf(8, 16, D), bf(8, 80, D), f32(8, 8, D),
            bf(8, 32, W), bf(8, 32, W), bf(2, 8, 32, D), bf(2, 8, 32, D), bf(2, 8, 32, D), bf(16, 4, 8, 16, D), bf(8, 80, D), f32(8, 8, D),
            f32(4, 64, 640), f32(4, 64, D), f32(10, 32, 16, D), bf(8, 32, W), f32(2, 8, 32, D), bf(2, 8, 32, D), bf(8, 48, D),
            bf(2, 8, 32, D), bf(3, 16, 8, 16, D), bf(3, 16, 8, 16, D), f32(4, 8, 16, D), bf(4, 3, 8, 16, D), bf(4, 3, 8, 16, D),
            bf(3, 8, 16, D), bf(3, 8, 16, D), bf(2, 8, 32, D), bf(8, 16, D),
            dma((11,)), dma((7, 7)), dma((7, 8)), dma((7,)), dma((2,)), dma((2,)),
            dma((7,)), dma((7,)), dma((8,)), dma((8,)), dma((16, 3)), dma((16, 3)),
            dma((5, 7)), dma((5, 8)), dma((5,)), dma, dma,
            dma((3,)), dma((3,)), dma((4, 3)), dma((4, 3)), dma((16, 3)), dma((16, 3)),
        ],
        compiler_params=pltpu.CompilerParams(collective_id=0, has_side_effects=True, vmem_limit_bytes=60 * 2**20),
        name="exchange_and_grads",
    )(*rows, *tables)
    return tuple(
        pl.pallas_call(
            finish_kernel,
            out_shape=shapes(
                ((32, 40 * D), BF), ((32, 8 * D), BF), ((32, 8 * D), BF),
                ((8, 40 * D), BF), ((8, 8 * D), BF), ((8, 8 * D), BF),
            ),
            in_specs=vmem(5),
            out_specs=vmem(6),
            name="finish",
        )(*landed)
    )


def solution(mesh):
    rows = P(("dp", "head"), None)
    return jax.shard_map(
        local,
        mesh=mesh,
        in_specs=(rows,) * 10 + (P(),) * 4,
        out_specs=(rows,) * 6,
        check_vma=False,
    )
```
